128 devices in a mesh: dp: 16 (over y_lo, z, core), tensor: 8 (over x, y_hi).
Axes of the slice: x: 4, y: 4 (y_hi: 2, y_lo: 2; y = y_hi * 2 + y_lo), z: 4, core: 2. Of those that a mesh axis runs over, the one named last changes fastest.
Arguments:
- query: bfloat16 [4, 2048, 4096], P(None, 'dp', 'tensor'), may hold values from -61 to 61
- new_keys: bfloat16 [4, 2048, 1024], P(None, 'dp', 'tensor'), may hold values from -6 to 6
- new_values: bfloat16 [4, 2048, 1024], P(None, 'dp', 'tensor'), may hold values from -6 to 6
- cache_keys: bfloat16 [2048, 64, 1024], P('dp', None, 'tensor'), may hold values from -3 to 3
- cache_values: bfloat16 [2048, 64, 1024], P('dp', None, 'tensor'), may hold values from -6 to 6
- cache_lengths: int32 [2048], P('dp'), may hold values from 2 to 64, as said below
- residual: bfloat16 [4, 2048, 8192], P(None, 'dp', 'tensor'), may hold values from -6 to 6
- out_weight: bfloat16 [4096, 8192], P('tensor'), may hold values from -0.09375 to 0.09375
- bridge_weight: bfloat16 [8192, 3584], P('tensor'), may hold values from -0.0625 to 0.0625
- text_table: bfloat16 [3584, 76032], P(('dp', 'tensor')), may hold values from -45 to 45
- codec_table: bfloat16 [3584, 8448], P(('dp', 'tensor')), may hold values from -45 to 45
- tokens: int32 [4, 2048], P(None, 'dp'), may hold values from 0 to 76031
- frames: int32 [4, 2048], P(None, 'dp'), may hold values from 0 to 8447
- talk_gain: bfloat16 [3584], replicated, may hold values from 0.099609375 to 1.8984375
Outputs:
- thinker_hidden: bfloat16 [4, 2048, 8192], P(None, 'dp', 'tensor')
- talker_input: bfloat16 [4, 2048, 3584], P(None, ('dp', 'tensor'))
The draws below stay inside these ranges and needn't reach their ends.
Inputs may be any that keep to these rules, and one draw needn't show every extreme that they name: `cache_lengths`: stream 0 has all 64 positions valid.
All inputs are finite; a program needn't handle non-finite values.
Results may differ from the reference program's by a relative error of at most 0.0035.
Values may be sent and summed in bfloat16 or wider, within the bound.
No kernel may reach another device: no remote copies, remote signals or barrier semaphores. Data moves between devices by JAX's collectives and lax.ppermute only.
A program may use at most 192 MiB of HBM per device.

```python
import math
import jax
import jax.numpy as jnp
import numpy as np
from jax import lax

D = 8192
QH = 32
KVH = 8
HD = 128
TW = 3584
VOCAB_W = 76032
CODEC = 8448
STEPS = 4
CAP = 64
STREAMS = 2048


def shared_keys(key):
    noise = jax.random.normal(key, (STREAMS, CAP, KVH * HD), jnp.float32)
    return jnp.clip(noise, -3.0, 3.0)


def table_scales(key, feats, entries):
    first, second = jax.random.split(key)
    lower = math.log(0.3)
    upper = math.log(3.0)
    feat_scale = jnp.exp(jax.random.uniform(first, (feats, 1), jnp.float32, lower, upper))
    entry_scale = jnp.exp(jax.random.uniform(second, (1, entries), jnp.float32, lower, upper))
    return feat_scale * entry_scale


def normal_values(key, feats, entries):
    return jnp.clip(jax.random.normal(key, (feats, entries), jnp.float32), -5.0, 5.0)


def draw_cache_keys(key, part):
    base = shared_keys(key)
    return base.astype(jnp.bfloat16)


def draw_query(key, part):
    key = jax.random.fold_in(key, 5)
    noise = jax.random.normal(key, (STEPS, STREAMS, QH * HD), jnp.float32)
    noise = jnp.clip(noise, -6.0, 6.0)
    return noise.astype(jnp.bfloat16)


def draw_text_table(key, part):
    key = jax.random.fold_in(key, 7)
    scale_key, value_key = jax.random.split(key)
    scales = table_scales(scale_key, TW, VOCAB_W)
    values = normal_values(value_key, TW, VOCAB_W)
    return (values * scales).astype(jnp.bfloat16)


def draw_codec_table(key, part):
    key = jax.random.fold_in(key, 11)
    scale_key, value_key = jax.random.split(key)
    scales = table_scales(scale_key, TW, CODEC)
    values = normal_values(value_key, TW, CODEC)
    return (values * scales).astype(jnp.bfloat16)


def draw_cache_lengths(key, part):
    key = jax.random.fold_in(key, 13)
    lengths = jax.random.randint(key, (STREAMS,), 2, CAP + 1, dtype=jnp.int32)
    return lengths.at[0].set(CAP)


def touch_ends(values, own_key, low, top_value):
    spot = [jax.random.randint(jax.random.fold_in(own_key, axis), (), 0, length) for axis, length in enumerate(values.shape)]
    main_axis = values.shape.index(max(values.shape))
    beside = spot[:main_axis] + [(spot[main_axis] + 1) % values.shape[main_axis]] + spot[main_axis + 1:]
    return values.at[tuple(spot)].set(low).at[tuple(beside)].set(top_value)


def block_scale(rng, extent, cuts, smallest, high):
    factor_of = 1.0
    for position, blocks in cuts:
        draws = jax.random.uniform(jax.random.fold_in(jax.random.fold_in(rng, 6), position), (blocks,), jnp.float32, smallest / len(cuts), high / len(cuts))
        factor_of = factor_of * jnp.repeat(jnp.exp(draws), extent[position] // blocks).reshape((-1,) + (1,) * (len(extent) - 1 - position))
    return factor_of


def skewed_wide(own_key, extent, amount, slope):
    weights = [min(1 << octave, amount + 1 - (1 << octave)) * (1 << 20) // math.isqrt((1 << octave) ** slope) + 1 for octave in range((amount + 1).bit_length()) if 1 << octave <= amount]
    scale = 1 + sum(weights) // (1 << 30)
    listing = np.cumsum(np.array([max(1, weight // scale) for weight in weights]))
    pick = jax.random.randint(jax.random.fold_in(own_key, 1), extent, 0, int(listing[len(weights) - 1]))
    start = jnp.left_shift(1, jnp.searchsorted(jnp.asarray(listing, jnp.int32), pick, side="right").astype(jnp.int32))
    standing = start - 1 + jax.random.randint(jax.random.fold_in(own_key, 4), extent, 0, 1 << 30) % jnp.minimum(start, amount + 1 - start)
    return jax.random.permutation(jax.random.fold_in(own_key, 2), amount)[standing].astype(jnp.int32)


def scatter_about(key, dims, width, limit, cuts=(), kind=jnp.bfloat16):
    drawn = jax.random.normal(key, dims, jnp.float32) * width
    if len(cuts) > 0:
        drawn = block_scale(key, dims, cuts, -0.22, 0.18) * drawn
    return jnp.clip(drawn, min=-limit, max=limit).astype(kind)


def setup_inputs(seed: int = 0) -> dict:
    streams_of = jax.random.split(jax.random.key(seed), 15)
    query = draw_query(jax.random.fold_in(streams_of[14], 71), 0)
    new_keys = scatter_about(streams_of[1], (STEPS, STREAMS, KVH * HD), 1.0, 6.0, ((1, 16), (2, 8)))
    new_values = scatter_about(streams_of[2], (STEPS, STREAMS, KVH * HD), 1.0, 6.0, ((1, 16), (2, 8)))
    cache_keys = draw_cache_keys(jax.random.fold_in(streams_of[14], 71), 0)
    cache_values = scatter_about(streams_of[4], (STREAMS, CAP, KVH * HD), 1.0, 6.0, ((0, 16), (2, 8)))
    cache_lengths = draw_cache_lengths(jax.random.fold_in(streams_of[14], 71), 0)
    residual = scatter_about(streams_of[6], (STEPS, STREAMS, D), 1.0, 6.0, ((1, 16), (2, 8)))
    out_weight = scatter_about(streams_of[7], (QH * HD, D), (QH * HD) ** -0.5, 0.09375, ((0, 8),))
    bridge_weight = scatter_about(streams_of[8], (D, TW), D ** -0.5, 0.0625, ((0, 8),))
    text_table = draw_text_table(jax.random.fold_in(streams_of[14], 71), 0)
    codec_table = draw_codec_table(jax.random.fold_in(streams_of[14], 71), 0)
    tokens = touch_ends(skewed_wide(streams_of[11], (STEPS, STREAMS), VOCAB_W, 2), jax.random.fold_in(streams_of[11], 3), 0, VOCAB_W - 1).astype(jnp.int32)
    frames = touch_ends(jax.random.randint(streams_of[12], (STEPS, STREAMS), 0, CODEC), jax.random.fold_in(streams_of[12], 1), 0, CODEC - 1).astype(jnp.int32)
    talk_gain = jnp.clip(1.0 + 0.18 * jax.random.normal(streams_of[13], (TW,), jnp.float32), 0.099609375, 1.8984375).astype(jnp.bfloat16)
    return dict(query=query, new_keys=new_keys, new_values=new_values, cache_keys=cache_keys, cache_values=cache_values, cache_lengths=cache_lengths, residual=residual, out_weight=out_weight, bridge_weight=bridge_weight, text_table=text_table, codec_table=codec_table, tokens=tokens, frames=frames, talk_gain=talk_gain)


def reference(query, new_keys, new_values, cache_keys, cache_values, cache_lengths, residual, out_weight, bridge_weight, text_table, codec_table, tokens, frames, talk_gain):
    group = QH // KVH
    scale = 1.0 / HD ** 0.5
    cached_k = cache_keys.reshape(STREAMS, CAP, KVH, HD).astype(jnp.float32)
    cached_v = cache_values.reshape(STREAMS, CAP, KVH, HD).astype(jnp.float32)
    fresh_k = new_keys.reshape(STEPS, STREAMS, KVH, HD).astype(jnp.float32)
    fresh_v = new_values.reshape(STEPS, STREAMS, KVH, HD).astype(jnp.float32)
    positions = jnp.arange(CAP, dtype=jnp.int32)
    valid = positions[None, :] < cache_lengths[:, None].astype(jnp.int32)
    hidden_rows = []
    talker_rows = []
    for step in range(STEPS):
        queries = query[step].reshape(STREAMS, KVH, group, HD).astype(jnp.float32)
        score_c = jnp.einsum('skgd,spkd->skgp', queries, cached_k) * scale
        score_c = jnp.where(valid[:, None, None, :], score_c, -1e+30)
        score_n = jnp.einsum('skgd,uskd->skgu', queries, fresh_k[:step + 1]) * scale
        top = jnp.maximum(lax.optimization_barrier(jnp.max(score_c, axis=-1)), lax.optimization_barrier(jnp.max(score_n, axis=-1)))[..., None]
        exp_c = jnp.exp(score_c - top)
        exp_n = jnp.exp(score_n - top)
        total = lax.optimization_barrier(jnp.sum(exp_c, axis=-1, keepdims=True)) + lax.optimization_barrier(jnp.sum(exp_n, axis=-1, keepdims=True))
        weight_c = (exp_c / total).astype(jnp.bfloat16).astype(jnp.float32)
        weight_n = (exp_n / total).astype(jnp.bfloat16).astype(jnp.float32)
        attended = jnp.einsum('skgp,spkd->skgd', weight_c, cached_v) + jnp.einsum('skgu,uskd->skgd', weight_n, fresh_v[:step + 1])
        attended = attended.astype(jnp.bfloat16).reshape(STREAMS, QH * HD)
        projected = jnp.dot(attended, out_weight, preferred_element_type=jnp.float32)
        hidden = (residual[step].astype(jnp.float32) + projected).astype(jnp.bfloat16)
        bridged = jnp.dot(hidden, bridge_weight, preferred_element_type=jnp.float32)
        text_rows = jnp.take(text_table, tokens[step], axis=1).T.astype(jnp.float32)
        codec_rows = jnp.take(codec_table, frames[step], axis=1).T.astype(jnp.float32)
        mixed = bridged + text_rows + codec_rows
        normed = mixed * lax.rsqrt(lax.optimization_barrier(jnp.mean(mixed * mixed, axis=-1, keepdims=True)) + 1e-06)
        talker_rows.append((normed * talk_gain.astype(jnp.float32)).astype(jnp.bfloat16))
        hidden_rows.append(hidden)
    return (jnp.stack(hidden_rows), jnp.stack(talker_rows))
```

```python
import functools

import jax
import jax.numpy as jnp
from jax import lax
from jax.experimental import pallas as pl
from jax.experimental.pallas import tpu as pltpu
from jax.sharding import PartitionSpec as P

QH = 32
KVH = 8
HD = 128
CAP = 64
GROUP = QH // KVH
STEPS = 4
SB = 16
LANES = 128
FPAD = 32
BF16 = jnp.bfloat16
F32 = jnp.float32
BOTH = ("dp", "tensor")
MIB = 1 << 20


def iota(shape, dim):
    return lax.broadcasted_iota(jnp.int32, shape, dim)


def attention_kernel(key_ref, q_ref, ck_ref, cv_ref, nk_ref, nv_ref, out_ref):
    rows = STEPS * GROUP * SB
    scale = 1.0 / HD**0.5
    queries = jnp.concatenate(
        [q_ref[t, :, h * HD : (h + 1) * HD] for t in range(STEPS) for h in range(GROUP)], axis=0
    )
    cached_k = ck_ref[...].reshape(SB * CAP, HD)
    cached_v = cv_ref[...].reshape(SB * CAP, HD)
    fresh_k = nk_ref[...].reshape(STEPS * SB, HD)
    fresh_v = nv_ref[...].reshape(STEPS * SB, HD)
    contract = (((1,), (1,)), ((), ()))
    score_c = lax.dot_general(queries, cached_k, contract, preferred_element_type=F32) * scale
    score_n = lax.dot_general(queries, fresh_k, contract, preferred_element_type=F32) * scale
    own = iota((rows, 1), 0) % SB
    score_c = jnp.where(own == key_ref[0], score_c, -1e30)
    row, col = iota((rows, STEPS * SB), 0), iota((rows, STEPS * SB), 1)
    seen = (row % SB == col % SB) & (col // SB <= row // (GROUP * SB))
    score_n = jnp.where(seen, score_n, -1e30)
    top = jnp.maximum(
        jnp.max(score_c, axis=-1, keepdims=True), jnp.max(score_n, axis=-1, keepdims=True)
    )
    exp_c = jnp.exp(score_c - top)
    exp_n = jnp.exp(score_n - top)
    total = jnp.sum(exp_c, axis=-1, keepdims=True) + jnp.sum(exp_n, axis=-1, keepdims=True)
    inverse = 1.0 / total
    weight_c = (exp_c * inverse).astype(BF16)
    weight_n = (exp_n * inverse).astype(BF16)
    attended = jnp.dot(weight_c, cached_v, preferred_element_type=F32)
    attended = attended + jnp.dot(weight_n, fresh_v, preferred_element_type=F32)
    attended = attended.astype(BF16)
    for t in range(STEPS):
        for h in range(GROUP):
            at = (t * GROUP + h) * SB
            out_ref[t, :, h * HD : (h + 1) * HD] = attended[at : at + SB]


def attention(query, new_keys, new_values, cache_keys, cache_values, cache_lengths):
    steps, streams, width = query.shape
    blocks = streams // SB
    position = jnp.arange(CAP, dtype=jnp.int32)[None, :]
    own = (jnp.arange(streams, dtype=jnp.int32) % SB)[:, None]
    keys = jnp.where(position < cache_lengths[:, None], own, -1).reshape(blocks, 1, SB * CAP)
    fresh = pl.BlockSpec((steps, SB, HD), lambda i: (0, i, 0))
    cached = pl.BlockSpec((SB, CAP, HD), lambda i: (i, 0, 0))
    heads = pl.BlockSpec((steps, SB, width), lambda i: (0, i, 0))
    return pl.pallas_call(
        attention_kernel,
        grid=(blocks,),
        in_specs=[
            pl.BlockSpec((1, 1, SB * CAP), lambda i: (i, 0, 0)),
            heads,
            cached,
            cached,
            fresh,
            fresh,
        ],
        out_specs=heads,
        out_shape=jax.ShapeDtypeStruct(query.shape, BF16),
        compiler_params=pltpu.CompilerParams(vmem_limit_bytes=32 * MIB),
        cost_estimate=pl.CostEstimate(
            flops=2 * 2 * 2048 * 1024 * 128 * 2, bytes_accessed=6 * MIB, transcendentals=2 * MIB
        ),
        name="attention",
    )(keys, query, cache_keys, cache_values, new_keys, new_values)


def embed_kernel(code_ref, text_ref, codec_ref, out_ref, text_s, codec_s):
    feats = text_ref.shape[0]

    def unpack(src, dst):
        def body(b, _):
            at = pl.multiple_of(b * LANES, LANES)
            block = src[:, pl.ds(at, LANES)].astype(F32)
            dst[b] = jnp.concatenate([block, jnp.zeros((FPAD - feats, LANES), F32)], axis=0)
            return 0

        lax.fori_loop(0, dst.shape[0], body, 0)

    unpack(text_ref, text_s)
    unpack(codec_ref, codec_s)
    lane = iota((FPAD, LANES), 1)

    def owner(o, _):
        acc = jnp.zeros((FPAD, LANES), F32)
        for j in range(LANES):
            code = code_ref[o, j]
            table = text_s if j < LANES // 2 else codec_s
            found = table[lax.shift_right_logical(code, 7)]
            found = pltpu.roll(found, code & (LANES - 1), 1)
            acc = jnp.where(lane == j, found, acc)
        out_ref[o] = acc.astype(BF16)
        return 0

    lax.fori_loop(0, out_ref.shape[0], owner, 0)


def embed(codes, text_table, codec_table):
    owners = codes.shape[0]
    vmem = pl.BlockSpec(memory_space=pltpu.VMEM)
    return pl.pallas_call(
        embed_kernel,
        in_specs=[pl.BlockSpec(memory_space=pltpu.SMEM), vmem, vmem],
        out_specs=vmem,
        out_shape=jax.ShapeDtypeStruct((owners, FPAD, LANES), BF16),
        scratch_shapes=[
            pltpu.VMEM((text_table.shape[1] // LANES, FPAD, LANES), F32),
            pltpu.VMEM((codec_table.shape[1] // LANES, FPAD, LANES), F32),
        ],
        compiler_params=pltpu.CompilerParams(vmem_limit_bytes=40 * MIB),
        cost_estimate=pl.CostEstimate(flops=40 * 1000 * 1000, bytes_accessed=100 * MIB, transcendentals=0),
        name="embed",
    )(codes, text_table, codec_table)


def project_kernel(a_ref, w_ref, res_ref, bridge_ref, hidden_ref, part_ref, acc, kept, *, owners):
    i = pl.program_id(0)

    @pl.when(i < owners)
    def _():
        w = w_ref[...].reshape(a_ref.shape[2], w_ref.shape[3])
        prod = jnp.dot(a_ref[0], w, preferred_element_type=F32)

        @pl.when(i == 0)
        def _():
            acc[...] = prod

        @pl.when(i > 0)
        def _():
            acc[...] += prod

    @pl.when(i == owners - 1)
    def _():
        hidden = (res_ref[...].astype(F32) + acc[...]).astype(BF16)
        kept[...] = hidden
        hidden_ref[...] = hidden

    @pl.when(i >= owners)
    def _():
        part = jnp.dot(kept[...], bridge_ref[...], preferred_element_type=F32).astype(BF16)
        per = part_ref.shape[2]
        width = part_ref.shape[3]
        part_ref[...] = (
            part.reshape(STEPS, owners, per, width).transpose(1, 0, 2, 3)
        )


def project(attended, weight, residual, bridge):
    owners, rows, depth = attended.shape
    parts, width = weight.shape[0], weight.shape[3]
    talk = bridge.shape[1]
    cols = 512
    first = lambda i: jnp.minimum(i, owners - 1)
    later = lambda i: jnp.maximum(i - owners, 0)
    whole = pl.BlockSpec((rows, width), lambda i: (0, 0))
    return pl.pallas_call(
        functools.partial(project_kernel, owners=owners),
        grid=(owners + talk // cols,),
        in_specs=[
            pl.BlockSpec((1, rows, depth), lambda i: (first(i), 0, 0)),
            pl.BlockSpec((parts, 1, depth // parts, width), lambda i: (0, first(i), 0, 0)),
            whole,
            pl.BlockSpec((width, cols), lambda i: (0, later(i))),
        ],
        out_specs=[
            whole,
            pl.BlockSpec((owners, STEPS, rows // STEPS // owners, cols), lambda i: (0, 0, 0, later(i))),
        ],
        out_shape=[
            jax.ShapeDtypeStruct((rows, width), BF16),
            jax.ShapeDtypeStruct((owners, STEPS, rows // STEPS // owners, talk), BF16),
        ],
        scratch_shapes=[pltpu.VMEM((rows, width), F32), pltpu.VMEM((rows, width), BF16)],
        compiler_params=pltpu.CompilerParams(vmem_limit_bytes=48 * MIB),
        cost_estimate=pl.CostEstimate(flops=8 * 10**9, bytes_accessed=24 * MIB, transcendentals=0),
        name="project",
    )(attended, weight, residual, bridge)


def finish_kernel(part_ref, emb_ref, gain_ref, out_ref, pick, mixed, square, *, feats):
    i = pl.program_id(0)
    sources, rows, cols = part_ref.shape
    depth = emb_ref.shape[0] * FPAD
    half = LANES // 2

    @pl.when(i == 0)
    def _():
        row = iota((depth, 1), 0)
        target = jnp.where(row % FPAD < feats, row // FPAD * feats + row % FPAD, -1)
        pick[...] = jnp.where(iota((depth, cols), 1) == target, 1.0, 0.0).astype(BF16)
        square[...] = jnp.zeros_like(square)

    total = part_ref[0].astype(F32)
    for s in range(1, sources):
        total = total + part_ref[s].astype(F32)
    found = lax.dot_general(
        emb_ref[...].reshape(depth, LANES),
        pick[...],
        (((0,), (0,)), ((), ())),
        preferred_element_type=F32,
    )
    total = total + found[:half] + found[half:]
    mixed[i] = total
    square[...] += jnp.sum(total * total, axis=-1, keepdims=True)

    @pl.when(i == pl.num_programs(0) - 1)
    def _():
        blocks = mixed.shape[0]
        factor = lax.rsqrt(square[...] * (1.0 / (blocks * cols)) + 1e-06)
        for b in range(blocks):
            gain = gain_ref[:, b * cols : (b + 1) * cols].astype(F32)
            out_ref[:, b * cols : (b + 1) * cols] = (mixed[b] * factor * gain).astype(BF16)


def finish(parts, emb, gain):
    sources, rows, talk = parts.shape
    feats = talk // emb.shape[0]
    blocks = 4
    cols = talk // blocks
    return pl.pallas_call(
        functools.partial(finish_kernel, feats=feats),
        grid=(blocks,),
        in_specs=[
            pl.BlockSpec((sources, rows, cols), lambda i: (0, 0, i)),
            pl.BlockSpec((emb.shape[0] // blocks, FPAD, LANES), lambda i: (i, 0, 0)),
            pl.BlockSpec((1, talk), lambda i: (0, 0)),
        ],
        out_specs=pl.BlockSpec((rows, talk), lambda i: (0, 0)),
        out_shape=jax.ShapeDtypeStruct((rows, talk), BF16),
        scratch_shapes=[
            pltpu.VMEM((emb.shape[0] // blocks * FPAD, cols), BF16),
            pltpu.VMEM((blocks, rows, cols), F32),
            pltpu.VMEM((rows, 1), F32),
        ],
        compiler_params=pltpu.CompilerParams(vmem_limit_bytes=32 * MIB),
        name="finish",
    )(parts, emb, gain)


def local(
    query,
    new_keys,
    new_values,
    cache_keys,
    cache_values,
    cache_lengths,
    residual,
    out_weight,
    bridge_weight,
    text_table,
    codec_table,
    tokens,
    frames,
    talk_gain,
):
    steps, streams, depth = query.shape
    width = residual.shape[2]
    talk = bridge_weight.shape[1]
    tensor = out_weight.shape[1] // width
    dp = lax.axis_size("dp")
    rows = steps * streams
    per = streams // tensor

    share = lax.dynamic_slice_in_dim(out_weight, lax.axis_index("dp") * (depth // dp), depth // dp, 0)
    share = share.reshape(depth // dp, tensor, width).transpose(1, 0, 2)
    share = lax.all_to_all(share, "tensor", 0, 0, tiled=True)
    weight = lax.all_gather(share, "dp")

    def by_owner(ids):
        return ids.reshape(steps, tensor, per).transpose(1, 0, 2).reshape(tensor, steps * per)

    ids = jnp.concatenate([by_owner(tokens), by_owner(frames)], axis=1)
    lane = jnp.arange(LANES, dtype=jnp.int32)[None, :]
    codes = (ids // LANES) * LANES + (lane - ids) % LANES
    codes = lax.all_gather(codes, "dp", axis=0, tiled=True)
    emb = embed(codes, text_table, codec_table)
    emb = lax.all_to_all(emb, BOTH, 0, 0, tiled=True)

    attended = attention(query, new_keys, new_values, cache_keys, cache_values, cache_lengths)
    attended = attended.reshape(rows, depth)
    attended = lax.all_to_all(
        jnp.broadcast_to(attended[None], (tensor, rows, depth)), "tensor", 0, 0, tiled=True
    )
    hidden, parts = project(attended, weight, residual.reshape(rows, width), bridge_weight)
    parts = lax.all_to_all(
        parts.reshape(tensor, steps * per, talk), "tensor", 0, 0, tiled=True
    )
    talker = finish(parts, emb, talk_gain.reshape(1, talk))
    return hidden.reshape(steps, streams, width), talker.reshape(steps, per, talk)


def solution(mesh):
    in_specs = (
        P(None, "dp", "tensor"),
        P(None, "dp", "tensor"),
        P(None, "dp", "tensor"),
        P("dp", None, "tensor"),
        P("dp", None, "tensor"),
        P("dp"),
        P(None, "dp", "tensor"),
        P("tensor", None),
        P("tensor", None),
        P(("dp", "tensor"), None),
        P(("dp", "tensor"), None),
        P(None, "dp"),
        P(None, "dp"),
        P(),
    )
    out_specs = (P(None, "dp", "tensor"), P(None, ("dp", "tensor"), None))
    return jax.shard_map(local, mesh=mesh, in_specs=in_specs, out_specs=out_specs, check_vma=False)
```

```python
import functools

import jax
import jax.numpy as jnp
from jax import lax
from jax.experimental import pallas as pl
from jax.experimental.pallas import tpu as pltpu
from jax.sharding import PartitionSpec as P

QH = 32
KVH = 8
HD = 128
CAP = 64
GROUP = QH // KVH
STEPS = 4
SB = 16
LANES = 128
FPAD = 32
PACK = LANES // FPAD
BF16 = jnp.bfloat16
F32 = jnp.float32
BOTH = ("dp", "tensor")
MIB = 1 << 20


def iota(shape, dim):
    return lax.broadcasted_iota(jnp.int32, shape, dim)


def attention_kernel(key_ref, q_ref, ck_ref, cv_ref, nk_ref, nv_ref, out_ref):
    rows = STEPS * GROUP * SB
    scale = 1.0 / HD**0.5
    queries = jnp.concatenate(
        [q_ref[t, :, h * HD : (h + 1) * HD] for t in range(STEPS) for h in range(GROUP)], axis=0
    )
    cached_k = ck_ref[...].reshape(SB * CAP, HD)
    cached_v = cv_ref[...].reshape(SB * CAP, HD)
    fresh_k = nk_ref[...].reshape(STEPS * SB, HD)
    fresh_v = nv_ref[...].reshape(STEPS * SB, HD)
    contract = (((1,), (1,)), ((), ()))
    score_c = lax.dot_general(queries, cached_k, contract, preferred_element_type=F32) * scale
    score_n = lax.dot_general(queries, fresh_k, contract, preferred_element_type=F32) * scale
    own = iota((rows, 1), 0) % SB
    score_c = jnp.where(own == key_ref[0], score_c, -1e30)
    row, col = iota((rows, STEPS * SB), 0), iota((rows, STEPS * SB), 1)
    seen = (row % SB == col % SB) & (col // SB <= row // (GROUP * SB))
    score_n = jnp.where(seen, score_n, -1e30)
    top = jnp.maximum(
        jnp.max(score_c, axis=-1, keepdims=True), jnp.max(score_n, axis=-1, keepdims=True)
    )
    exp_c = jnp.exp(score_c - top)
    exp_n = jnp.exp(score_n - top)
    total = jnp.sum(exp_c, axis=-1, keepdims=True) + jnp.sum(exp_n, axis=-1, keepdims=True)
    inverse = 1.0 / total
    weight_c = (exp_c * inverse).astype(BF16)
    weight_n = (exp_n * inverse).astype(BF16)
    attended = jnp.dot(weight_c, cached_v, preferred_element_type=F32)
    attended = attended + jnp.dot(weight_n, fresh_v, preferred_element_type=F32)
    attended = attended.astype(BF16)
    for t in range(STEPS):
        for h in range(GROUP):
            at = (t * GROUP + h) * SB
            out_ref[t, :, h * HD : (h + 1) * HD] = attended[at : at + SB]


def attention(query, new_keys, new_values, cache_keys, cache_values, cache_lengths):
    steps, streams, width = query.shape
    blocks = streams // SB
    position = jnp.arange(CAP, dtype=jnp.int32)[None, :]
    own = (jnp.arange(streams, dtype=jnp.int32) % SB)[:, None]
    keys = jnp.where(position < cache_lengths[:, None], own, -1).reshape(blocks, 1, SB * CAP)
    fresh = pl.BlockSpec((steps, SB, HD), lambda i: (0, i, 0))
    cached = pl.BlockSpec((SB, CAP, HD), lambda i: (i, 0, 0))
    heads = pl.BlockSpec((steps, SB, width), lambda i: (0, i, 0))
    return pl.pallas_call(
        attention_kernel,
        grid=(blocks,),
        in_specs=[
            pl.BlockSpec((1, 1, SB * CAP), lambda i: (i, 0, 0)),
            heads,
            cached,
            cached,
            fresh,
            fresh,
        ],
        out_specs=heads,
        out_shape=jax.ShapeDtypeStruct(query.shape, BF16),
        compiler_params=pltpu.CompilerParams(vmem_limit_bytes=32 * MIB),
        cost_estimate=pl.CostEstimate(
            flops=2 * 2 * 2048 * 1024 * 128 * 2, bytes_accessed=6 * MIB, transcendentals=2 * MIB
        ),
        name="attention",
    )(keys, query, cache_keys, cache_values, new_keys, new_values)


def turn_kernel(text_ref, codec_ref, text_out, codec_out):
    feats = text_ref.shape[0]
    pad = jnp.zeros((FPAD - feats, LANES), F32)

    def turn(src, dst):
        blocks = src.shape[1] // LANES

        def rows(first, count):
            parts = []
            for k in range(count):
                at = pl.multiple_of((first + k) * LANES, LANES)
                parts += [src[:, pl.ds(at, LANES)].astype(F32), pad]
            if count < PACK:
                parts.append(jnp.zeros(((PACK - count) * FPAD, LANES), F32))
            return jnp.concatenate(parts, axis=0).T

        def body(g, _):
            dst[pl.ds(pl.multiple_of(g * LANES, LANES), LANES), :] = rows(g * PACK, PACK)
            return 0

        whole = blocks // PACK
        lax.fori_loop(0, whole, body, 0, unroll=4)
        if blocks % PACK:
            dst[whole * LANES : (whole + 1) * LANES, :] = rows(whole * PACK, blocks % PACK)

    turn(text_ref, text_out)
    turn(codec_ref, codec_out)


def turn_tables(text_table, codec_table):
    vmem = pl.BlockSpec(memory_space=pltpu.VMEM)
    rows = lambda table: pl.cdiv(table.shape[1], PACK * LANES) * LANES
    return pl.pallas_call(
        turn_kernel,
        in_specs=[vmem, vmem],
        out_specs=[vmem, vmem],
        out_shape=[jax.ShapeDtypeStruct((rows(t), LANES), F32) for t in (text_table, codec_table)],
        compiler_params=pltpu.CompilerParams(vmem_limit_bytes=40 * MIB),
        cost_estimate=pl.CostEstimate(flops=0, bytes_accessed=16 * MIB, transcendentals=0),
        name="turn_tables",
    )(text_table, codec_table)


def embed_kernel(code_ref, text_ref, codec_ref, out_ref, text_s, codec_s):
    half = code_ref.shape[1] // 2
    slot = iota((1, LANES), 1) // FPAD
    lane = iota((half // 2, LANES), 1)

    def look(table, code):
        row = table[pl.ds(lax.shift_right_logical(code, 2), 1), :]
        return jnp.where(slot == (code & (PACK - 1)), row, 0.0)

    def spread(x):
        x = x + pltpu.roll(x, 64, 1)
        return x + pltpu.roll(x, 32, 1)

    def owner(o, _):
        for r in range(half):
            text_s[r : r + 1, :] = look(text_ref, code_ref[o, r])
            codec_s[r : r + 1, :] = look(codec_ref, code_ref[o, half + r])
        text, codec = spread(text_s[...]), spread(codec_s[...])
        low = jnp.where(lane < FPAD, text[: half // 2], codec[: half // 2])
        high = jnp.where(lane < 3 * FPAD, text[half // 2 :], codec[half // 2 :])
        out_ref[o] = jnp.where(lane < 2 * FPAD, low, high).astype(BF16)
        return 0

    lax.fori_loop(0, out_ref.shape[0], owner, 0)


def embed(codes, text_rows, codec_rows):
    owners = codes.shape[0]
    vmem = pl.BlockSpec(memory_space=pltpu.VMEM)
    return pl.pallas_call(
        embed_kernel,
        in_specs=[pl.BlockSpec(memory_space=pltpu.SMEM), vmem, vmem],
        out_specs=vmem,
        out_shape=jax.ShapeDtypeStruct((owners, codes.shape[1] // 4, LANES), BF16),
        scratch_shapes=[pltpu.VMEM((codes.shape[1] // 2, LANES), F32)] * 2,
        compiler_params=pltpu.CompilerParams(vmem_limit_bytes=40 * MIB),
        cost_estimate=pl.CostEstimate(flops=0, bytes_accessed=owners * 256 * 1024, transcendentals=0),
        name="embed",
    )(codes, text_rows, codec_rows)


def project_kernel(order_ref, *refs, owners):
    del order_ref
    a_refs = refs[:owners]
    w_ref, res_ref, bridge_ref, hidden_ref, part_ref, acc, kept = refs[owners:]
    i = pl.program_id(0)
    depth = a_refs[0].shape[1]

    for k in range(owners):

        @pl.when(i == k)
        def _(k=k):
            w = w_ref[...].reshape(depth, w_ref.shape[3])
            prod = jnp.dot(a_refs[k][...], w, preferred_element_type=F32)
            if k == 0:
                acc[...] = res_ref[...].astype(F32) + prod
            elif k < owners - 1:
                acc[...] += prod
            else:
                hidden = (acc[...] + prod).astype(BF16)
                kept[...] = hidden
                hidden_ref[...] = hidden

    @pl.when(i >= owners)
    def _():
        at = pl.multiple_of((i - owners) * part_ref.shape[3], part_ref.shape[3])
        bridge = bridge_ref[:, pl.ds(at, part_ref.shape[3])]
        part = jnp.dot(kept[...], bridge, preferred_element_type=F32).astype(BF16)
        per = part_ref.shape[2]
        width = part_ref.shape[3]
        part_ref[...] = part.reshape(STEPS, owners, per, width).transpose(1, 0, 2, 3)


def project(attended, order, weight, residual, bridge):
    owners = len(attended)
    rows, depth = attended[0].shape
    parts, width = weight.shape[0], weight.shape[3]
    talk = bridge.shape[1]
    cols = 512
    first = lambda i: jnp.minimum(i, owners - 1)
    later = lambda i: jnp.maximum(i - owners, 0)
    vmem = pl.BlockSpec(memory_space=pltpu.VMEM)
    per = rows // STEPS // owners
    return pl.pallas_call(
        functools.partial(project_kernel, owners=owners),
        grid_spec=pltpu.PrefetchScalarGridSpec(
            num_scalar_prefetch=1,
            grid=(owners + talk // cols,),
            in_specs=[vmem] * owners
            + [
                pl.BlockSpec((parts, 1, depth // parts, width), lambda i, o: (0, o[first(i)], 0, 0)),
                vmem,
                vmem,
            ],
            out_specs=[
                pl.BlockSpec((rows, width), lambda i, o: (0, 0)),
                pl.BlockSpec((owners, STEPS, per, cols), lambda i, o: (0, 0, 0, later(i))),
            ],
            scratch_shapes=[pltpu.VMEM((rows, width), F32), pltpu.VMEM((rows, width), BF16)],
        ),
        out_shape=[
            jax.ShapeDtypeStruct((rows, width), BF16),
            jax.ShapeDtypeStruct((owners, STEPS, per, talk), BF16),
        ],
        compiler_params=pltpu.CompilerParams(vmem_limit_bytes=52 * MIB),
        cost_estimate=pl.CostEstimate(flops=8 * 10**9, bytes_accessed=24 * MIB, transcendentals=0),
        name="project",
    )(order, *attended, weight, residual, bridge)


def finish_kernel(part_ref, emb_ref, gain_ref, out_ref, mixed, square, *, feats):
    i = pl.program_id(0)
    sources, rows, cols = part_ref.shape
    holders, half, _ = emb_ref.shape

    @pl.when(i == 0)
    def _():
        square[...] = jnp.zeros_like(square)

    lane = iota((half, LANES), 1)
    found = [[jnp.zeros((half, LANES), F32)] * (cols // LANES) for _ in range(2)]
    for h in range(holders):
        both = emb_ref[h].astype(F32)
        both = both + pltpu.roll(both, LANES - FPAD, 1)
        tile, at = divmod(h * feats, LANES)
        end = at + feats
        for k in range(2):
            moved = pltpu.roll(both, (at - k * LANES // 2) % LANES, 1)
            inside = (lane >= at) & (lane < end)
            found[k][tile] = jnp.where(inside, moved, found[k][tile])
            if end > LANES:
                found[k][tile + 1] = jnp.where(lane < end - LANES, moved, found[k][tile + 1])
    total = part_ref[0].astype(F32)
    for s in range(1, sources):
        total = total + part_ref[s].astype(F32)
    total = total + jnp.concatenate([jnp.concatenate(f, axis=1) for f in found], axis=0)
    mixed[i] = total
    square[...] += jnp.sum(total * total, axis=-1, keepdims=True)

    @pl.when(i == pl.num_programs(0) - 1)
    def _():
        blocks = mixed.shape[0]
        factor = lax.rsqrt(square[...] * (1.0 / (blocks * cols)) + 1e-06)
        for b in range(blocks):
            gain = gain_ref[:, b * cols : (b + 1) * cols].astype(F32)
            out_ref[:, b * cols : (b + 1) * cols] = (mixed[b] * factor * gain).astype(BF16)


def finish(parts, emb, gain):
    sources, rows, talk = parts.shape
    feats = talk // emb.shape[0]
    blocks = 4
    cols = talk // blocks
    return pl.pallas_call(
        functools.partial(finish_kernel, feats=feats),
        grid=(blocks,),
        in_specs=[
            pl.BlockSpec((sources, rows, cols), lambda i: (0, 0, i)),
            pl.BlockSpec((emb.shape[0] // blocks,) + emb.shape[1:], lambda i: (i, 0, 0)),
            pl.BlockSpec((1, talk), lambda i: (0, 0)),
        ],
        out_specs=pl.BlockSpec((rows, talk), lambda i: (0, 0)),
        out_shape=jax.ShapeDtypeStruct((rows, talk), BF16),
        scratch_shapes=[
            pltpu.VMEM((blocks, rows, cols), F32),
            pltpu.VMEM((rows, 1), F32),
        ],
        compiler_params=pltpu.CompilerParams(vmem_limit_bytes=32 * MIB),
        name="finish",
    )(parts, emb, gain)


def gather_tensor(own):
    size = lax.axis_size("tensor")
    send = lambda x, pairs: lax.ppermute(x, "tensor", pairs)
    up = [(i, (i + 2) % size) for i in range(size)]
    down = [(i, (i - 2) % size) for i in range(size)]
    across = [(i, i ^ 1) for i in range(size)]
    half = own.shape[0] // 2
    from_up, from_down, beside = send(own, up), send(own, down), send(own, across)
    far = jnp.concatenate([send(from_up[:half], up), send(from_down[half:], down)], axis=0)
    beside_up, beside_down = send(beside, up), send(beside, down)
    beside_far = send(far, across)
    me = lax.axis_index("tensor")
    x, y = me // 2, me % 2
    spot = lambda k, other: (x + k) % (size // 2) * 2 + (y + other) % 2
    order = [spot(k, other) for k in (0, 3, 1, 2) for other in (0, 1)]
    arrays = [own, beside, from_up, beside_up, from_down, beside_down, far, beside_far]
    return arrays, jnp.stack(order).astype(jnp.int32)


def local(
    query,
    new_keys,
    new_values,
    cache_keys,
    cache_values,
    cache_lengths,
    residual,
    out_weight,
    bridge_weight,
    text_table,
    codec_table,
    tokens,
    frames,
    talk_gain,
):
    steps, streams, depth = query.shape
    width = residual.shape[2]
    talk = bridge_weight.shape[1]
    tensor = out_weight.shape[1] // width
    dp = lax.axis_size("dp")
    rows = steps * streams
    per = streams // tensor

    share = lax.dynamic_slice_in_dim(out_weight, lax.axis_index("dp") * (depth // dp), depth // dp, 0)
    share = share.reshape(depth // dp, tensor, width).transpose(1, 0, 2)

    def by_owner(ids):
        ids = ids.reshape(steps, tensor, per).transpose(1, 0, 2).reshape(tensor, steps * per)
        block, lane = ids // LANES, ids % LANES
        return (block // PACK * LANES + lane) * PACK + block % PACK

    codes = jnp.concatenate([by_owner(tokens), by_owner(frames)], axis=1)
    codes = lax.all_to_all(jnp.broadcast_to(codes[None], (dp,) + codes.shape), "dp", 0, 0, tiled=True)
    codes = codes.reshape(dp * tensor, codes.shape[2])
    share = lax.all_to_all(share, "tensor", 0, 0, tiled=True)
    weight = lax.all_gather(share, "dp")
    text_rows, codec_rows = turn_tables(text_table, codec_table)

    attended = attention(query, new_keys, new_values, cache_keys, cache_values, cache_lengths)
    attended, codes, share = lax.optimization_barrier((attended, codes, share))
    attended, order = gather_tensor(attended.reshape(rows, depth))
    chunks = 4
    emb = [
        embed(c, text_rows, codec_rows) for c in jnp.split(codes, chunks, axis=0)
    ]
    emb = lax.all_to_all(jnp.concatenate(emb, axis=0), BOTH, 0, 0, tiled=True)
    hidden, parts = project(attended, order, weight, residual.reshape(rows, width), bridge_weight)
    parts = lax.all_to_all(
        parts.reshape(tensor, steps * per, talk), "tensor", 0, 0, tiled=True
    )
    talker = finish(parts, emb, talk_gain.reshape(1, talk))
    return hidden.reshape(steps, streams, width), talker.reshape(steps, per, talk)


def solution(mesh):
    in_specs = (
        P(None, "dp", "tensor"),
        P(None, "dp", "tensor"),
        P(None, "dp", "tensor"),
        P("dp", None, "tensor"),
        P("dp", None, "tensor"),
        P("dp"),
        P(None, "dp", "tensor"),
        P("tensor", None),
        P("tensor", None),
        P(("dp", "tensor"), None),
        P(("dp", "tensor"), None),
        P(None, "dp"),
        P(None, "dp"),
        P(),
    )
    out_specs = (P(None, "dp", "tensor"), P(None, ("dp", "tensor"), None))
    return jax.shard_map(local, mesh=mesh, in_specs=in_specs, out_specs=out_specs, check_vma=False)
```

```python
import functools

import jax
import jax.numpy as jnp
from jax import lax
from jax.experimental import pallas as pl
from jax.experimental.pallas import tpu as pltpu
from jax.sharding import PartitionSpec as P

QH = 32
KVH = 8
HD = 128
CAP = 64
GROUP = QH // KVH
STEPS = 4
SB = 16
LANES = 128
FPAD = 32
PACK = LANES // FPAD
BF16 = jnp.bfloat16
F32 = jnp.float32
BOTH = ("dp", "tensor")
MIB = 1 << 20


def iota(shape, dim):
    return lax.broadcasted_iota(jnp.int32, shape, dim)


def attention_kernel(len_ref, q_ref, ck_ref, cv_ref, nk_ref, nv_ref, out_ref):
    rows = STEPS * GROUP * SB
    scale = 1.0 / HD**0.5
    queries = jnp.concatenate(
        [q_ref[t, :, h * HD : (h + 1) * HD] for t in range(STEPS) for h in range(GROUP)], axis=0
    )
    cached_k = ck_ref[...].reshape(SB * CAP, HD)
    cached_v = cv_ref[...].reshape(SB * CAP, HD)
    fresh_k = nk_ref[...].reshape(STEPS * SB, HD)
    fresh_v = nv_ref[...].reshape(STEPS * SB, HD)
    contract = (((1,), (1,)), ((), ()))
    score_c = lax.dot_general(queries, cached_k, contract, preferred_element_type=F32) * scale
    score_n = lax.dot_general(queries, fresh_k, contract, preferred_element_type=F32) * scale
    own = iota((rows, 1), 0) % SB
    start = own * CAP
    stop = start + jnp.concatenate([len_ref[:, :1]] * (STEPS * GROUP), axis=0)
    spot = iota((rows, SB * CAP), 1)
    score_c = jnp.where((spot >= start) & (spot < stop), score_c, -1e30)
    row, col = iota((rows, STEPS * SB), 0), iota((rows, STEPS * SB), 1)
    seen = (row % SB == col % SB) & (col // SB <= row // (GROUP * SB))
    score_n = jnp.where(seen, score_n, -1e30)
    top = jnp.maximum(
        jnp.max(score_c, axis=-1, keepdims=True), jnp.max(score_n, axis=-1, keepdims=True)
    )
    exp_c = jnp.exp(score_c - top)
    exp_n = jnp.exp(score_n - top)
    total = jnp.sum(exp_c, axis=-1, keepdims=True) + jnp.sum(exp_n, axis=-1, keepdims=True)
    inverse = 1.0 / total
    weight_c = (exp_c * inverse).astype(BF16)
    weight_n = (exp_n * inverse).astype(BF16)
    attended = jnp.dot(weight_c, cached_v, preferred_element_type=F32)
    attended = attended + jnp.dot(weight_n, fresh_v, preferred_element_type=F32)
    attended = attended.astype(BF16)
    for t in range(STEPS):
        for h in range(GROUP):
            at = (t * GROUP + h) * SB
            out_ref[0, t, :, h * HD : (h + 1) * HD] = attended[at : at + SB]


def attention(query, new_keys, new_values, cache_keys, cache_values, cache_lengths):
    steps, streams, width = query.shape
    blocks = streams // SB
    lengths = jnp.broadcast_to(cache_lengths[:, None], (streams, LANES))
    fresh = pl.BlockSpec((steps, SB, HD), lambda i: (0, i, 0))
    cached = pl.BlockSpec((SB, CAP, HD), lambda i: (i, 0, 0))
    return pl.pallas_call(
        attention_kernel,
        grid=(blocks,),
        in_specs=[
            pl.BlockSpec((SB, LANES), lambda i: (i, 0)),
            pl.BlockSpec((steps, SB, width), lambda i: (0, i, 0)),
            cached,
            cached,
            fresh,
            fresh,
        ],
        out_specs=pl.BlockSpec((1, steps, SB, width), lambda i: (i, 0, 0, 0)),
        out_shape=jax.ShapeDtypeStruct((blocks, steps, SB, width), BF16),
        compiler_params=pltpu.CompilerParams(vmem_limit_bytes=32 * MIB),
        cost_estimate=pl.CostEstimate(flops=8 * 10**9, bytes_accessed=6 * MIB, transcendentals=0),
        name="attention",
    )(lengths, query, cache_keys, cache_values, new_keys, new_values)


def look_kernel(shift_ref, id_ref, table_ref, *refs, group):
    other_ref = refs[0] if len(refs) == 4 else None
    out_ref, turned, found = refs[-3:]
    feats, entries = table_ref.shape
    owners = out_ref.shape[0]
    rows = 2 * out_ref.shape[1]
    per = rows // STEPS
    batch = found.shape[0] // rows
    pad = jnp.zeros((FPAD - feats, LANES), BF16)
    slot = iota((LANES, LANES), 1) // FPAD

    def turn(first, count):
        parts = []
        for k in range(count):
            at = pl.multiple_of((first + k) * LANES, LANES)
            parts += [table_ref[:, pl.ds(at, LANES)], pad]
        if count < PACK:
            parts.append(jnp.zeros(((PACK - count) * FPAD, LANES), BF16))
        packed = jnp.concatenate(parts, axis=0).T.astype(F32)
        for k in range(count):
            at = pl.multiple_of((first + k) * LANES, LANES)
            turned[pl.ds(at, LANES), :] = jnp.where(slot == k, packed, 0.0)

    def turn_units(i, _):
        for u in range(4):
            turn((i * 4 + u) * PACK, PACK)
        return 0

    blocks = entries // LANES
    loops = blocks // (4 * PACK)
    lax.fori_loop(0, loops, turn_units, 0)
    for first in range(loops * 4 * PACK, blocks, PACK):
        turn(first, min(PACK, blocks - first))

    place = (iota((LANES, LANES), 1) - shift_ref[0]) & (LANES - 1)
    row = iota((LANES, LANES), 0)
    move = (row % FPAD == place % FPAD) & (place // FPAD % 2 == group)
    move = jnp.where(move, 1.0, 0.0).astype(BF16)
    place = (iota((rows // 2, LANES), 1) - shift_ref[0]) & (LANES - 1)

    def look(i, _):
        def find(j, _):
            o = i * batch + j
            base = o // (LANES // per) * (STEPS * LANES) + o % (LANES // per) * per
            to = pl.multiple_of(j * rows, rows)
            for t in range(STEPS):
                for s in range(per):
                    at = id_ref[base + (t * LANES + s)]
                    found[pl.ds(to + (t * per + s), 1), :] = turned[pl.ds(at, 1), :]
            return 0

        lax.fori_loop(0, batch, find, 0)
        moved = jnp.dot(found[...].astype(BF16), move, preferred_element_type=F32)
        for j in range(batch):
            a = moved[j * rows : j * rows + rows // 2]
            b = moved[j * rows + rows // 2 : (j + 1) * rows]
            both = jnp.where(place < 2 * FPAD, a, b)
            if other_ref is not None:
                both = both + other_ref[i * batch + j].astype(F32)
            out_ref[i * batch + j] = both.astype(BF16)
        return 0

    lax.fori_loop(0, owners // batch, look, 0)


def look_up(ids, table, shift, owners, group, *other):
    groups, _, streams = ids.shape
    rows = streams * STEPS // owners
    vmem = pl.BlockSpec(memory_space=pltpu.VMEM)
    smem = pl.BlockSpec(memory_space=pltpu.SMEM)
    return pl.pallas_call(
        functools.partial(look_kernel, group=group),
        in_specs=[smem, smem, vmem] + [vmem] * len(other),
        out_specs=vmem,
        out_shape=jax.ShapeDtypeStruct((groups * owners, rows // 2, LANES), BF16),
        scratch_shapes=[
            pltpu.VMEM((table.shape[1], LANES), F32),
            pltpu.VMEM((8 * rows, LANES), F32),
        ],
        compiler_params=pltpu.CompilerParams(vmem_limit_bytes=(table.shape[1] // 2048 + 14) * MIB),
        cost_estimate=pl.CostEstimate(
            flops=0, bytes_accessed=(20 + table.shape[1] // 3000) * MIB, transcendentals=0
        ),
        name="look_up",
    )(shift, ids.reshape(-1), table, *other)


def project_kernel(order_ref, subs_ref, *refs, owners):
    a_refs = refs[:owners]
    *w_refs, res_ref, bridge_ref, hidden_ref, part_ref, a_all, w_all = refs[owners:]
    depth = a_refs[0].shape[1]
    cols = w_all.shape[2]
    for k in range(owners):
        at = pl.multiple_of(order_ref[k] * depth, depth)
        a_all[:, pl.ds(at, depth)] = a_refs[k][...]

    def columns(n, _):
        here = pl.ds(pl.multiple_of(n * cols, cols), cols)
        sub = 0
        for w_ref in w_refs:
            for k in range(w_ref.shape[1]):
                size = w_ref.shape[2]
                at = pl.multiple_of(subs_ref[sub] * size, size)
                w_all[:, pl.ds(at, size), :] = w_ref[:, k, :, here]
                sub += 1
        w = w_all[...].reshape(owners * depth, cols)
        prod = jnp.dot(a_all[...], w, preferred_element_type=F32)
        hidden_ref[:, here] = (res_ref[:, here].astype(F32) + prod).astype(BF16)
        return 0

    lax.fori_loop(0, hidden_ref.shape[1] // cols, columns, 0)
    wide = 512

    def bridge(n, _):
        here = pl.ds(pl.multiple_of(n * wide, wide), wide)
        part = jnp.dot(hidden_ref[...], bridge_ref[:, here], preferred_element_type=F32)
        part_ref[:, here] = part.astype(BF16)
        return 0

    lax.fori_loop(0, part_ref.shape[1] // wide, bridge, 0)


def project(attended, order, weights, subs, residual, bridge):
    owners = len(attended)
    rows, depth = attended[0].shape
    vmem = pl.BlockSpec(memory_space=pltpu.VMEM)
    smem = pl.BlockSpec(memory_space=pltpu.SMEM)
    return pl.pallas_call(
        functools.partial(project_kernel, owners=owners),
        in_specs=[smem, smem] + [vmem] * (owners + len(weights) + 2),
        out_specs=[vmem, vmem],
        out_shape=[
            jax.ShapeDtypeStruct(residual.shape, BF16),
            jax.ShapeDtypeStruct((rows, bridge.shape[1]), BF16),
        ],
        scratch_shapes=[
            pltpu.VMEM((rows, owners * depth), BF16),
            pltpu.VMEM((owners, depth, 256), BF16),
        ],
        compiler_params=pltpu.CompilerParams(vmem_limit_bytes=48 * MIB),
        cost_estimate=pl.CostEstimate(flops=12 * 10**9, bytes_accessed=24 * MIB, transcendentals=0),
        name="project",
    )(order, subs, *attended, *weights, residual, bridge)


def place_kernel(emb_ref, out_ref, *, feats):
    holders, half, _ = emb_ref.shape
    lane = iota((half, LANES), 1)
    for tile in range(holders * feats // LANES):
        start = tile * LANES
        found = [jnp.zeros((half, LANES), F32) for _ in range(PACK)]
        for h in range(start // feats, min((start + LANES - 1) // feats, holders - 1) + 1):
            row = emb_ref[h].astype(F32)
            low, high = max(h * feats - start, 0), min((h + 1) * feats - start, LANES)
            for g in range(PACK):
                spot = (lane - g * FPAD) & (LANES - 1)
                found[g] = jnp.where((spot >= low) & (spot < high), row, found[g])
        a = found[0] + pltpu.roll(found[1], LANES - FPAD, 1)
        b = found[2] + pltpu.roll(found[3], LANES - FPAD, 1)
        b = pltpu.roll(b, LANES // 2, 1)
        out_ref[:half, start : start + LANES] = a
        out_ref[half:, start : start + LANES] = b


def place(emb, talk):
    holders, half, _ = emb.shape
    blocks = 4
    return pl.pallas_call(
        functools.partial(place_kernel, feats=talk // holders),
        grid=(blocks,),
        in_specs=[pl.BlockSpec((holders // blocks, half, LANES), lambda i: (i, 0, 0))],
        out_specs=pl.BlockSpec((2 * half, talk // blocks), lambda i: (0, i)),
        out_shape=jax.ShapeDtypeStruct((2 * half, talk), F32),
        cost_estimate=pl.CostEstimate(flops=0, bytes_accessed=8 * MIB, transcendentals=0),
        name="place",
    )(emb)


def finish_kernel(part_ref, emb_ref, gain_ref, out_ref, mixed):
    sources, rows, talk = part_ref.shape
    square = jnp.zeros((rows, LANES), F32)
    for c in range(talk // LANES):
        cols = slice(c * LANES, (c + 1) * LANES)
        total = part_ref[0, :, cols].astype(F32)
        for s in range(1, sources):
            total = total + part_ref[s, :, cols].astype(F32)
        total = total + emb_ref[:, cols]
        mixed[:, cols] = total
        square = square + total * total
    mean = jnp.sum(square, axis=-1, keepdims=True) * (1.0 / talk)
    factor = lax.rsqrt(mean + 1e-06)
    for c in range(talk // LANES):
        cols = slice(c * LANES, (c + 1) * LANES)
        gain = gain_ref[:, cols].astype(F32)
        out_ref[:, cols] = (mixed[:, cols] * factor * gain).astype(BF16)


def finish(parts, emb, gain):
    _, rows, talk = parts.shape
    vmem = pl.BlockSpec(memory_space=pltpu.VMEM)
    return pl.pallas_call(
        finish_kernel,
        in_specs=[vmem, vmem, vmem],
        out_specs=vmem,
        out_shape=jax.ShapeDtypeStruct((rows, talk), BF16),
        scratch_shapes=[pltpu.VMEM((rows, talk), F32)],
        compiler_params=pltpu.CompilerParams(vmem_limit_bytes=32 * MIB),
        cost_estimate=pl.CostEstimate(flops=0, bytes_accessed=8 * MIB, transcendentals=0),
        name="finish",
    )(parts, emb, gain)


def tensor_pairs():
    size = lax.axis_size("tensor")
    up = [(i, (i + 2) % size) for i in range(size)]
    down = [(i, (i - 2) % size) for i in range(size)]
    return up, down, [(i, i ^ 1) for i in range(size)]


def send(x, pairs):
    return lax.ppermute(x, "tensor", pairs)


def gather_first(own):
    up, down, across = tensor_pairs()
    return send(own, up), send(own, down), send(own, across)


def gather_second(own, first):
    up, down, _ = tensor_pairs()
    from_up, from_down, beside = first
    half = own.shape[0] // 2
    far = jnp.concatenate([send(from_up[:half], up), send(from_down[half:], down)], axis=0)
    return [own, beside, from_up, send(beside, up), from_down, send(beside, down), far]


def gather_third(second):
    size = lax.axis_size("tensor")
    arrays = second + [send(second[-1], tensor_pairs()[2])]
    me = lax.axis_index("tensor")
    x, y = me // 2, me % 2
    spot = lambda k, other: (x + k) % (size // 2) * 2 + (y + other) % 2
    order = [spot(k, other) for k in (0, 3, 1, 2) for other in (0, 1)]
    return arrays, jnp.stack(order).astype(jnp.int32)


def share_kernel(subs_ref, w_ref, out_ref, sems):
    owners, parts, size, width = out_ref.shape
    copies = []
    for k in range(parts):
        rows = pl.ds(pl.multiple_of(subs_ref[k] * size, size), size)
        for t in range(owners):
            copies.append(
                pltpu.make_async_copy(
                    w_ref.at[rows, t * width : (t + 1) * width], out_ref.at[t, k], sems.at[t, k]
                )
            )
    for copy in copies:
        copy.start()
    for copy in copies:
        copy.wait()


def share_rows(out_weight, subs, size, width):
    owners = out_weight.shape[1] // width
    return pl.pallas_call(
        share_kernel,
        in_specs=[pl.BlockSpec(memory_space=pltpu.SMEM), pl.BlockSpec(memory_space=pl.ANY)],
        out_specs=pl.BlockSpec(memory_space=pltpu.VMEM),
        out_shape=jax.ShapeDtypeStruct((owners, subs.shape[0], size, width), BF16),
        scratch_shapes=[pltpu.SemaphoreType.DMA((owners, subs.shape[0]))],
        compiler_params=pltpu.CompilerParams(vmem_limit_bytes=16 * MIB),
        cost_estimate=pl.CostEstimate(flops=0, bytes_accessed=4 * MIB, transcendentals=0),
        name="share_rows",
    )(subs, out_weight)


def weight_first(out_weight, width):
    depth = out_weight.shape[0]
    tensor = out_weight.shape[1] // width
    size = depth // 8
    me = lax.axis_index("dp")
    core, odd = me % 2, me // 2 % 2
    sub_a, sub_b = core * 4 + odd, core * 4 + 3 - odd
    pair = jnp.stack([sub_a, sub_b]).astype(jnp.int32)
    share = lax.all_to_all(share_rows(out_weight, pair, size, width), "tensor", 0, 0, tiled=True)

    own = [sub_a, sub_b, core * 4 + 1 - odd, core * 4 + 2 + odd]
    return share, jnp.stack(own + [(k + 4) % 8 for k in own]).astype(jnp.int32)


def weight_second(share):
    count = lax.axis_size("dp")
    turn = lambda i, by: i // 8 * 8 + (i + 2 * by) % 8
    z_of = lambda i: i // 2 % 4
    pairs_a = [(i, turn(i, -1 if z_of(i) % 2 else 1)) for i in range(count)]
    pairs_b = [(i, turn(i, 1 if z_of(i) % 2 else -1)) for i in range(count)]
    beside_a = lax.ppermute(share[:, :1], "dp", pairs_a)
    beside_b = lax.ppermute(share[:, 1:], "dp", pairs_b)
    return [share, beside_a, beside_b]


def weight_third(weights):
    cores = [(i, i ^ 1) for i in range(lax.axis_size("dp"))]
    return weights + [lax.ppermute(x, "dp", cores) for x in weights]


def local(
    query,
    new_keys,
    new_values,
    cache_keys,
    cache_values,
    cache_lengths,
    residual,
    out_weight,
    bridge_weight,
    text_table,
    codec_table,
    tokens,
    frames,
    talk_gain,
):
    steps, streams, depth = query.shape
    width = residual.shape[2]
    talk = bridge_weight.shape[1]
    tensor = out_weight.shape[1] // width
    dp = lax.axis_size("dp")
    rows = steps * streams
    per = streams // tensor

    share, subs = weight_first(out_weight, width)
    ids = jnp.concatenate([tokens, frames], axis=0)
    ids = lax.all_to_all(jnp.broadcast_to(ids[None], (dp,) + ids.shape), "dp", 0, 0, tiled=True)
    feats = text_table.shape[0]
    shift = (lax.axis_index("dp") * tensor + lax.axis_index("tensor")) * feats % LANES
    shift = shift[None].astype(jnp.int32)

    attended = attention(query, new_keys, new_values, cache_keys, cache_values, cache_lengths)
    attended = attended.reshape(rows, depth)
    first = gather_first(attended)
    codec = look_up(ids[:, steps:], codec_table, shift, tensor, 1)
    first, codec, share = lax.optimization_barrier((first, codec, share))
    second = gather_second(attended, first)
    weights = weight_second(share)
    emb = look_up(ids[:, :steps], text_table, shift, tensor, 0, codec)
    second, weights, emb = lax.optimization_barrier((second, weights, emb))
    attended, order = gather_third(second)
    weights = weight_third(weights)
    emb = lax.all_to_all(emb, BOTH, 0, 0, tiled=True)
    mine = residual.reshape(steps, tensor, per, width).transpose(1, 0, 2, 3).reshape(rows, width)
    hidden, parts = project(attended, order, weights, subs, mine, bridge_weight)
    parts = lax.all_to_all(parts.reshape(tensor, steps * per, talk), "tensor", 0, 0, tiled=True)
    talker = finish(parts, place(emb, talk), talk_gain.reshape(1, talk))
    hidden = hidden.reshape(tensor, steps, per, width).transpose(1, 0, 2, 3)
    return hidden.reshape(steps, streams, width), talker.reshape(steps, per, talk)


def solution(mesh):
    in_specs = (
        P(None, "dp", "tensor"),
        P(None, "dp", "tensor"),
        P(None, "dp", "tensor"),
        P("dp", None, "tensor"),
        P("dp", None, "tensor"),
        P("dp"),
        P(None, "dp", "tensor"),
        P("tensor", None),
        P("tensor", None),
        P(("dp", "tensor"), None),
        P(("dp", "tensor"), None),
        P(None, "dp"),
        P(None, "dp"),
        P(),
    )
    out_specs = (P(None, "dp", "tensor"), P(None, ("dp", "tensor"), None))
    return jax.shard_map(local, mesh=mesh, in_specs=in_specs, out_specs=out_specs, check_vma=False)
```

```python
import functools

import jax
import jax.numpy as jnp
from jax import lax
from jax.experimental import pallas as pl
from jax.experimental.pallas import tpu as pltpu
from jax.sharding import PartitionSpec as P

QH = 32
KVH = 8
HD = 128
CAP = 64
GROUP = QH // KVH
STEPS = 4
SB = 16
LANES = 128
FPAD = 32
PACK = LANES // FPAD
BF16 = jnp.bfloat16
F32 = jnp.float32
BOTH = ("dp", "tensor")
MIB = 1 << 20


def iota(shape, dim):
    return lax.broadcasted_iota(jnp.int32, shape, dim)


def attention_kernel(len_ref, q_ref, ck_ref, cv_ref, nk_ref, nv_ref, out_ref):
    rows = STEPS * GROUP * SB
    scale = 1.0 / HD**0.5
    queries = jnp.concatenate(
        [q_ref[t, :, h * HD : (h + 1) * HD] for t in range(STEPS) for h in range(GROUP)], axis=0
    )
    cached_k = ck_ref[...].reshape(SB * CAP, HD)
    cached_v = cv_ref[...].reshape(SB * CAP, HD)
    fresh_k = nk_ref[...].reshape(STEPS * SB, HD)
    fresh_v = nv_ref[...].reshape(STEPS * SB, HD)
    contract = (((1,), (1,)), ((), ()))
    score_c = lax.dot_general(queries, cached_k, contract, preferred_element_type=F32) * scale
    score_n = lax.dot_general(queries, fresh_k, contract, preferred_element_type=F32) * scale
    own = iota((rows, 1), 0) % SB
    start = own * CAP
    stop = start + jnp.concatenate([len_ref[:, :1]] * (STEPS * GROUP), axis=0)
    spot = iota((rows, SB * CAP), 1)
    score_c = jnp.where((spot >= start) & (spot < stop), score_c, -1e30)
    row, col = iota((rows, STEPS * SB), 0), iota((rows, STEPS * SB), 1)
    seen = (row % SB == col % SB) & (col // SB <= row // (GROUP * SB))
    score_n = jnp.where(seen, score_n, -1e30)
    top = jnp.maximum(
        jnp.max(score_c, axis=-1, keepdims=True), jnp.max(score_n, axis=-1, keepdims=True)
    )
    exp_c = jnp.exp(score_c - top)
    exp_n = jnp.exp(score_n - top)
    total = jnp.sum(exp_c, axis=-1, keepdims=True) + jnp.sum(exp_n, axis=-1, keepdims=True)
    inverse = 1.0 / total
    weight_c = (exp_c * inverse).astype(BF16)
    weight_n = (exp_n * inverse).astype(BF16)
    attended = jnp.dot(weight_c, cached_v, preferred_element_type=F32)
    attended = attended + jnp.dot(weight_n, fresh_v, preferred_element_type=F32)
    attended = attended.astype(BF16)
    for t in range(STEPS):
        for h in range(GROUP):
            at = (t * GROUP + h) * SB
            out_ref[0, t, :, h * HD : (h + 1) * HD] = attended[at : at + SB]


def attention(query, new_keys, new_values, cache_keys, cache_values, cache_lengths):
    steps, streams, width = query.shape
    blocks = streams // SB
    lengths = jnp.broadcast_to(cache_lengths[:, None], (streams, LANES))
    fresh = pl.BlockSpec((steps, SB, HD), lambda i: (0, i, 0))
    cached = pl.BlockSpec((SB, CAP, HD), lambda i: (i, 0, 0))
    return pl.pallas_call(
        attention_kernel,
        grid=(blocks,),
        in_specs=[
            pl.BlockSpec((SB, LANES), lambda i: (i, 0)),
            pl.BlockSpec((steps, SB, width), lambda i: (0, i, 0)),
            cached,
            cached,
            fresh,
            fresh,
        ],
        out_specs=pl.BlockSpec((1, steps, SB, width), lambda i: (i, 0, 0, 0)),
        out_shape=jax.ShapeDtypeStruct((blocks, steps, SB, width), BF16),
        compiler_params=pltpu.CompilerParams(vmem_limit_bytes=58 * MIB),
        cost_estimate=pl.CostEstimate(flops=8 * 10**9, bytes_accessed=6 * MIB, transcendentals=0),
        name="attention",
    )(lengths, query, cache_keys, cache_values, new_keys, new_values)


def look_kernel(shift_ref, spot_ref, id_ref, table_ref, *refs, group):
    other_ref = refs[0] if len(refs) == 4 else None
    out_ref, turned, found = refs[-3:]
    feats, entries = table_ref.shape
    owners = out_ref.shape[0]
    rows = 2 * out_ref.shape[1]
    per = rows // STEPS
    batch = found.shape[0] // rows
    pad = jnp.zeros((FPAD - feats, LANES), BF16)
    slot = iota((LANES, LANES), 1) // FPAD

    def turn(first, count):
        parts = []
        for k in range(count):
            at = pl.multiple_of((first + k) * LANES, LANES)
            parts += [table_ref[:, pl.ds(at, LANES)], pad]
        if count < PACK:
            parts.append(jnp.zeros(((PACK - count) * FPAD, LANES), BF16))
        packed = jnp.concatenate(parts, axis=0).T.astype(F32)
        for k in range(count):
            at = pl.multiple_of((first + k) * LANES, LANES)
            turned[pl.ds(at, LANES), :] = jnp.where(slot == k, packed, 0.0)

    def turn_units(i, _):
        for u in range(4):
            turn((i * 4 + u) * PACK, PACK)
        return 0

    blocks = entries // LANES
    loops = blocks // (4 * PACK)
    lax.fori_loop(0, loops, turn_units, 0)
    for first in range(loops * 4 * PACK, blocks, PACK):
        turn(first, min(PACK, blocks - first))

    place = (iota((LANES, LANES), 1) - shift_ref[0]) & (LANES - 1)
    row = iota((LANES, LANES), 0)
    move = (row % FPAD == place % FPAD) & (place // FPAD % 2 == group)
    move = jnp.where(move, 1.0, 0.0).astype(BF16)
    place = (iota((rows // 2, LANES), 1) - shift_ref[0]) & (LANES - 1)

    def look(i, _):
        def find(j, _):
            o = i * batch + j
            base = spot_ref[o // (LANES // per)] + o % (LANES // per) * per
            to = pl.multiple_of(j * rows, rows)
            for t in range(STEPS):
                for s in range(per):
                    at = id_ref[base + ((group * STEPS + t) * LANES + s)]
                    found[pl.ds(to + (t * per + s), 1), :] = turned[pl.ds(at, 1), :]
            return 0

        lax.fori_loop(0, batch, find, 0)
        moved = jnp.dot(found[...].astype(BF16), move, preferred_element_type=F32)
        for j in range(batch):
            a = moved[j * rows : j * rows + rows // 2]
            b = moved[j * rows + rows // 2 : (j + 1) * rows]
            both = jnp.where(place < 2 * FPAD, a, b)
            if other_ref is not None:
                both = both + other_ref[i * batch + j].astype(F32)
            out_ref[i * batch + j] = both.astype(BF16)
        return 0

    lax.fori_loop(0, owners // batch, look, 0)


def look_up(ids, group, spots, table, shift, owners, *other):
    groups, _, streams = ids.shape
    rows = streams * STEPS // owners
    vmem = pl.BlockSpec(memory_space=pltpu.VMEM)
    smem = pl.BlockSpec(memory_space=pltpu.SMEM)
    return pl.pallas_call(
        functools.partial(look_kernel, group=group),
        in_specs=[smem, smem, smem, vmem] + [vmem] * len(other),
        out_specs=vmem,
        out_shape=jax.ShapeDtypeStruct((groups * owners, rows // 2, LANES), BF16),
        scratch_shapes=[
            pltpu.VMEM((table.shape[1], LANES), F32),
            pltpu.VMEM((8 * rows, LANES), F32),
        ],
        compiler_params=pltpu.CompilerParams(vmem_limit_bytes=(table.shape[1] // 2048 + 14) * MIB),
        cost_estimate=pl.CostEstimate(
            flops=0, bytes_accessed=(20 + table.shape[1] // 3000) * MIB, transcendentals=0
        ),
        name="look_up",
    )(shift, spots, ids.reshape(-1), table, *other)


def collect_rows_kernel(order_ref, *refs, owners):
    a_refs = refs[:owners]
    res_ref, a_all, res_all, done, a_sem, res_sem = refs[owners:]
    depth = a_refs[0].shape[1]
    copies = []
    for t in range(STEPS):
        copies.append(pltpu.make_async_copy(res_ref.at[t], res_all.at[:, t], res_sem.at[t]))
    for k in range(owners):
        at = pl.multiple_of(order_ref[k] * depth, depth)
        copies.append(pltpu.make_async_copy(a_refs[k], a_all.at[:, pl.ds(at, depth)], a_sem.at[k]))
    for copy in copies:
        copy.start()
    for copy in copies:
        copy.wait()
    done[...] = jnp.zeros_like(done)


def collect_rows(attended, order, residual):
    owners = len(attended)
    rows, depth = attended[0].shape
    width = residual.shape[-1]
    vmem = pl.BlockSpec(memory_space=pltpu.VMEM)
    return pl.pallas_call(
        functools.partial(collect_rows_kernel, owners=owners),
        in_specs=[pl.BlockSpec(memory_space=pltpu.SMEM)]
        + [pl.BlockSpec(memory_space=pl.ANY)] * (owners + 1),
        out_specs=[vmem] * 3,
        out_shape=[
            jax.ShapeDtypeStruct((rows, owners * depth), BF16),
            jax.ShapeDtypeStruct((owners, STEPS, rows // STEPS // owners, width), BF16),
            jax.ShapeDtypeStruct((8, LANES), F32),
        ],
        scratch_shapes=[pltpu.SemaphoreType.DMA((n,)) for n in (owners, STEPS)],
        compiler_params=pltpu.CompilerParams(vmem_limit_bytes=12 * MIB),
        cost_estimate=pl.CostEstimate(flops=0, bytes_accessed=8 * MIB, transcendentals=0),
        name="collect_rows",
    )(order, *attended, residual)


def collect_weight_kernel(subs_ref, done_ref, *refs):
    del done_ref
    *w_refs, w_all, sems = refs
    copies = []
    for w_ref in w_refs:
        for k in range(w_ref.shape[1]):
            sub = len(copies)
            copies.append(
                pltpu.make_async_copy(w_ref.at[:, k], w_all.at[:, subs_ref[sub]], sems.at[sub])
            )
    for copy in copies:
        copy.start()
    for copy in copies:
        copy.wait()


def collect_weight(weights, subs, done):
    owners, _, size, width = weights[0].shape
    parts = subs.shape[0]
    return pl.pallas_call(
        collect_weight_kernel,
        in_specs=[pl.BlockSpec(memory_space=pltpu.SMEM)]
        + [pl.BlockSpec(memory_space=pl.ANY)] * (len(weights) + 1),
        out_specs=pl.BlockSpec(memory_space=pltpu.VMEM),
        out_shape=jax.ShapeDtypeStruct((owners, parts, size, width), BF16),
        scratch_shapes=[pltpu.SemaphoreType.DMA((parts,))],
        compiler_params=pltpu.CompilerParams(vmem_limit_bytes=12 * MIB),
        cost_estimate=pl.CostEstimate(flops=0, bytes_accessed=10 * MIB, transcendentals=0),
        name="collect_weight",
    )(subs, done, *weights)


def place_kernel(emb_ref, out_ref, *, feats):
    holders, half, _ = emb_ref.shape
    lane = iota((half, LANES), 1)
    for tile in range(holders * feats // LANES):
        start = tile * LANES
        found = [jnp.zeros((half, LANES), F32) for _ in range(PACK)]
        for h in range(start // feats, min((start + LANES - 1) // feats, holders - 1) + 1):
            row = emb_ref[h].astype(F32)
            low, high = max(h * feats - start, 0), min((h + 1) * feats - start, LANES)
            for g in range(PACK):
                spot = (lane - g * FPAD) & (LANES - 1)
                found[g] = jnp.where((spot >= low) & (spot < high), row, found[g])
        a = found[0] + pltpu.roll(found[1], LANES - FPAD, 1)
        b = found[2] + pltpu.roll(found[3], LANES - FPAD, 1)
        b = pltpu.roll(b, LANES // 2, 1)
        out_ref[:half, start : start + LANES] = a
        out_ref[half:, start : start + LANES] = b


def place(emb, talk):
    holders, half, _ = emb.shape
    blocks = 4
    return pl.pallas_call(
        functools.partial(place_kernel, feats=talk // holders),
        grid=(blocks,),
        in_specs=[pl.BlockSpec((holders // blocks, half, LANES), lambda i: (i, 0, 0))],
        out_specs=pl.BlockSpec((2 * half, talk // blocks), lambda i: (0, i)),
        out_shape=jax.ShapeDtypeStruct((2 * half, talk), F32),
        cost_estimate=pl.CostEstimate(flops=0, bytes_accessed=8 * MIB, transcendentals=0),
        name="place",
    )(emb)


def finish_kernel(part_ref, emb_ref, gain_ref, out_ref, mixed):
    sources, rows, talk = part_ref.shape
    square = jnp.zeros((rows, LANES), F32)
    for c in range(talk // LANES):
        cols = slice(c * LANES, (c + 1) * LANES)
        total = part_ref[0, :, cols].astype(F32)
        for s in range(1, sources):
            total = total + part_ref[s, :, cols].astype(F32)
        total = total + emb_ref[:, cols]
        mixed[:, cols] = total
        square = square + total * total
    mean = jnp.sum(square, axis=-1, keepdims=True) * (1.0 / talk)
    factor = lax.rsqrt(mean + 1e-06)
    for c in range(talk // LANES):
        cols = slice(c * LANES, (c + 1) * LANES)
        gain = gain_ref[:, cols].astype(F32)
        out_ref[:, cols] = (mixed[:, cols] * factor * gain).astype(BF16)


def finish(parts, emb, gain):
    _, rows, talk = parts.shape
    vmem = pl.BlockSpec(memory_space=pltpu.VMEM)
    return pl.pallas_call(
        finish_kernel,
        in_specs=[vmem, vmem, vmem],
        out_specs=vmem,
        out_shape=jax.ShapeDtypeStruct((rows, talk), BF16),
        scratch_shapes=[pltpu.VMEM((rows, talk), F32)],
        compiler_params=pltpu.CompilerParams(vmem_limit_bytes=32 * MIB),
        cost_estimate=pl.CostEstimate(flops=0, bytes_accessed=8 * MIB, transcendentals=0),
        name="finish",
    )(parts, emb, gain)


def gather_ids(ids, share, later):
    count = lax.axis_size("dp")
    size = ids.size
    get = lambda x, peer: lax.ppermute(x, "dp", [(peer(i), i) for i in range(count)])
    turn = lambda by: lambda i: i // 8 * 8 + (i + 2 * by) % 8
    across_y, share = lax.optimization_barrier((get(ids, lambda i: i ^ 8), share))
    ids = jnp.stack([ids, across_y])
    ids = jnp.concatenate([ids, get(ids, lambda i: i ^ 1)])
    ids, later = lax.optimization_barrier((ids, later))
    ids = jnp.concatenate([ids] + [get(ids, turn(by)) for by in (1, 2, 3)])
    me = lax.axis_index("dp")
    peer = jnp.arange(count, dtype=jnp.int32)
    across = (peer // 2 - me // 2) % 4
    other = (peer % 2 != me % 2) * 2 + (peer // 8 != me // 8)
    return share, later, ids, ((across * 4 + other) * size).astype(jnp.int32)


def tensor_pairs():
    size = lax.axis_size("tensor")
    along = lambda by: [(i, (i + 2 * by) % size) for i in range(size)]
    return along(1), along(-1), along(2), [(i, i ^ 1) for i in range(size)]


def send(x, pairs):
    return lax.ppermute(x, "tensor", pairs)


def gather_first(own):
    return [send(own, pairs) for pairs in tensor_pairs()]


def gather_second(first):
    up, down, _, across = tensor_pairs()
    _, _, far, beside = first
    return [send(beside, up), send(beside, down), send(far, across)]


def peers_order():
    size = lax.axis_size("tensor")
    me = lax.axis_index("tensor")
    x, y = me // 2, me % 2
    spot = lambda k, other: (x + k) % (size // 2) * 2 + (y + other) % 2
    order = [(0, 0), (3, 0), (1, 0), (2, 0), (0, 1), (3, 1), (1, 1), (2, 1)]
    return jnp.stack([spot(*o) for o in order]).astype(jnp.int32)


def share_kernel(subs_ref, w_ref, out_ref, sems):
    owners, parts, size, width = out_ref.shape
    copies = []
    for k in range(parts):
        rows = pl.ds(pl.multiple_of(subs_ref[k] * size, size), size)
        for t in range(owners):
            copies.append(
                pltpu.make_async_copy(
                    w_ref.at[rows, t * width : (t + 1) * width], out_ref.at[t, k], sems.at[t, k]
                )
            )
    for copy in copies:
        copy.start()
    for copy in copies:
        copy.wait()


def share_rows(out_weight, subs, size, width):
    owners = out_weight.shape[1] // width
    return pl.pallas_call(
        share_kernel,
        in_specs=[pl.BlockSpec(memory_space=pltpu.SMEM), pl.BlockSpec(memory_space=pltpu.HBM)],
        out_specs=pl.BlockSpec(memory_space=pltpu.VMEM),
        out_shape=jax.ShapeDtypeStruct((owners, subs.shape[0], size, width), BF16),
        scratch_shapes=[pltpu.SemaphoreType.DMA((owners, subs.shape[0]))],
        compiler_params=pltpu.CompilerParams(vmem_limit_bytes=58 * MIB),
        cost_estimate=pl.CostEstimate(flops=0, bytes_accessed=4 * MIB, transcendentals=0),
        name="share_rows",
    )(subs, out_weight)


def weight_first(out_weight, width):
    depth = out_weight.shape[0]
    tensor = out_weight.shape[1] // width
    size = depth // 8
    me = lax.axis_index("dp")
    core, odd = me % 2, me // 2 % 2
    sub_a, sub_b = core * 4 + odd, core * 4 + 3 - odd
    pair = jnp.stack([sub_a, sub_b]).astype(jnp.int32)
    share = share_rows(out_weight, pair, size, width)

    own = [sub_a, sub_b, core * 4 + 1 - odd, core * 4 + 2 + odd]
    return share, jnp.stack(own + [(k + 4) % 8 for k in own]).astype(jnp.int32)


def weight_second(share):
    count = lax.axis_size("dp")
    turn = lambda i, by: i // 8 * 8 + (i + 2 * by) % 8
    z_of = lambda i: i // 2 % 4
    pairs_a = [(i, turn(i, -1 if z_of(i) % 2 else 1)) for i in range(count)]
    pairs_b = [(i, turn(i, 1 if z_of(i) % 2 else -1)) for i in range(count)]
    beside_a = lax.ppermute(share[:, :1], "dp", pairs_a)
    beside_b = lax.ppermute(share[:, 1:], "dp", pairs_b)
    return [share, beside_a, beside_b]


def weight_third(weights):
    cores = [(i, i ^ 1) for i in range(lax.axis_size("dp"))]
    return weights + [lax.ppermute(x, "dp", cores) for x in weights]


def local(
    query,
    new_keys,
    new_values,
    cache_keys,
    cache_values,
    cache_lengths,
    residual,
    out_weight,
    bridge_weight,
    text_table,
    codec_table,
    tokens,
    frames,
    talk_gain,
):
    steps, streams, depth = query.shape
    width = residual.shape[2]
    talk = bridge_weight.shape[1]
    tensor = out_weight.shape[1] // width
    dp = lax.axis_size("dp")
    rows = steps * streams
    per = streams // tensor

    feats = text_table.shape[0]
    shift = (lax.axis_index("dp") * tensor + lax.axis_index("tensor")) * feats % LANES
    shift = shift[None].astype(jnp.int32)
    share, subs = weight_first(out_weight, width)
    ids = jnp.concatenate([tokens, frames], axis=0)
    share, query, ids, spots = gather_ids(ids, share, query)
    share = lax.all_to_all(share, "tensor", 0, 0, tiled=True)

    attended = attention(query, new_keys, new_values, cache_keys, cache_values, cache_lengths)
    attended, ids = lax.optimization_barrier((attended.reshape(rows, depth), ids))
    first = gather_first(attended)
    text = look_up(ids, 0, spots, text_table, shift, tensor)
    first, text, share = lax.optimization_barrier((first, text, share))
    weights = weight_second(share)
    attended = [attended] + first + gather_second(first)
    emb = look_up(ids, 1, spots, codec_table, shift, tensor, text)
    residual = residual.reshape(steps, tensor, per, width)
    attended, mine, done = collect_rows(attended, peers_order(), residual)
    weights, done, emb = lax.optimization_barrier((weights, done, emb))
    emb = lax.all_to_all(emb, BOTH, 0, 0, tiled=True)
    weight = collect_weight(weight_third(weights), subs, done)
    hidden = jnp.dot(attended, weight.reshape(tensor * depth, width), preferred_element_type=F32)
    hidden = (mine.reshape(rows, width).astype(F32) + hidden).astype(BF16)
    parts = jnp.dot(hidden, bridge_weight, preferred_element_type=F32).astype(BF16)
    parts = lax.all_to_all(parts.reshape(tensor, steps * per, talk), "tensor", 0, 0, tiled=True)
    talker = finish(parts, place(emb, talk), talk_gain.reshape(1, talk))
    hidden = hidden.reshape(tensor, steps, per, width).transpose(1, 0, 2, 3)
    return hidden.reshape(steps, streams, width), talker.reshape(steps, per, talk)


def solution(mesh):
    in_specs = (
        P(None, "dp", "tensor"),
        P(None, "dp", "tensor"),
        P(None, "dp", "tensor"),
        P("dp", None, "tensor"),
        P("dp", None, "tensor"),
        P("dp"),
        P(None, "dp", "tensor"),
        P("tensor", None),
        P("tensor", None),
        P(("dp", "tensor"), None),
        P(("dp", "tensor"), None),
        P(None, "dp"),
        P(None, "dp"),
        P(),
    )
    out_specs = (P(None, "dp", "tensor"), P(None, ("dp", "tensor"), None))
    return jax.shard_map(local, mesh=mesh, in_specs=in_specs, out_specs=out_specs, check_vma=False)
```

```python
import functools

import jax
import jax.numpy as jnp
from jax import lax
from jax.experimental import pallas as pl
from jax.experimental.pallas import tpu as pltpu
from jax.sharding import PartitionSpec as P

QH = 32
KVH = 8
HD = 128
CAP = 64
GROUP = QH // KVH
STEPS = 4
SB = 16
BLOCKS = 2
LANES = 128
FPAD = 32
PACK = LANES // FPAD
BF16 = jnp.bfloat16
F32 = jnp.float32
BOTH = ("dp", "tensor")
MIB = 1 << 20


def iota(shape, dim):
    return lax.broadcasted_iota(jnp.int32, shape, dim)


def attention_kernel(len_ref, q_ref, ck_ref, cv_ref, nk_ref, nv_ref, out_ref):
    some = SB // 2
    rows = STEPS * GROUP * some
    scale = 1.0 / HD**0.5
    contract = (((1,), (1,)), ((), ()))
    query = [
        q_ref[t, :, h * HD : (h + 1) * HD].astype(F32) for t in range(STEPS) for h in range(GROUP)
    ]
    fresh = [[ref[t].astype(F32) for t in range(STEPS)] for ref in (nk_ref, nv_ref)]
    own = iota((rows, 1), 0) % some
    start = own * CAP
    spot = iota((rows, some * CAP), 1)
    row, col = iota((rows, STEPS * some), 0), iota((rows, STEPS * some), 1)
    seen = (row % some == col % some) & (col // some <= row // (GROUP * some))
    results = []
    for part in range(2 * BLOCKS):
        here = slice(part * some, (part + 1) * some)
        queries = jnp.concatenate([q[here] for q in query], axis=0).astype(BF16)
        cached_k = ck_ref[here].reshape(some * CAP, HD)
        cached_v = cv_ref[here].reshape(some * CAP, HD)
        fresh_k, fresh_v = [jnp.concatenate([x[here] for x in f], axis=0).astype(BF16) for f in fresh]
        score_c = lax.dot_general(queries, cached_k, contract, preferred_element_type=F32) * scale
        score_n = lax.dot_general(queries, fresh_k, contract, preferred_element_type=F32) * scale
        stop = start + jnp.concatenate([len_ref[here, :1]] * (STEPS * GROUP), axis=0)
        score_c = jnp.where((spot >= start) & (spot < stop), score_c, -1e30)
        score_n = jnp.where(seen, score_n, -1e30)
        top = jnp.maximum(
            jnp.max(score_c, axis=-1, keepdims=True), jnp.max(score_n, axis=-1, keepdims=True)
        )
        exp_c = jnp.exp(score_c - top)
        exp_n = jnp.exp(score_n - top)
        total = jnp.sum(exp_c, axis=-1, keepdims=True) + jnp.sum(exp_n, axis=-1, keepdims=True)
        inverse = 1.0 / total
        weight_c = (exp_c * inverse).astype(BF16)
        weight_n = (exp_n * inverse).astype(BF16)
        attended = jnp.dot(weight_c, cached_v, preferred_element_type=F32)
        results.append(attended + jnp.dot(weight_n, fresh_v, preferred_element_type=F32))
    for t in range(STEPS):
        for h in range(GROUP):
            at = (t * GROUP + h) * some
            for b in range(BLOCKS):
                both = [r[at : at + some] for r in results[2 * b : 2 * b + 2]]
                both = jnp.concatenate(both, axis=0).astype(BF16)
                out_ref[b, t, :, h * HD : (h + 1) * HD] = both


def attention(query, new_keys, new_values, cache_keys, cache_values, cache_lengths):
    steps, streams, width = query.shape
    blocks = streams // SB
    lengths = jnp.broadcast_to(cache_lengths[:, None], (streams, LANES))
    fresh = pl.BlockSpec((steps, BLOCKS * SB, HD), lambda i: (0, i, 0))
    cached = pl.BlockSpec((BLOCKS * SB, CAP, HD), lambda i: (i, 0, 0))
    return pl.pallas_call(
        attention_kernel,
        grid=(blocks // BLOCKS,),
        in_specs=[
            pl.BlockSpec((BLOCKS * SB, LANES), lambda i: (i, 0)),
            pl.BlockSpec((steps, BLOCKS * SB, width), lambda i: (0, i, 0)),
            cached,
            cached,
            fresh,
            fresh,
        ],
        out_specs=pl.BlockSpec((BLOCKS, steps, SB, width), lambda i: (i, 0, 0, 0)),
        out_shape=jax.ShapeDtypeStruct((blocks, steps, SB, width), BF16),
        compiler_params=pltpu.CompilerParams(vmem_limit_bytes=58 * MIB),
        cost_estimate=pl.CostEstimate(flops=8 * 10**9, bytes_accessed=6 * MIB, transcendentals=0),
        name="attention",
    )(lengths, query, cache_keys, cache_values, new_keys, new_values)


def look_kernel(shift_ref, spot_ref, id_ref, table_ref, *refs, group):
    other_ref = refs[0] if len(refs) == 4 else None
    out_ref, turned, found = refs[-3:]
    feats, entries = table_ref.shape
    owners = out_ref.shape[0]
    rows = 2 * out_ref.shape[1]
    per = rows // STEPS
    batch = found.shape[0] // rows
    pad = jnp.zeros((FPAD - feats, LANES), BF16)
    slot = iota((LANES, LANES), 1) // FPAD

    def turn(first, count):
        parts = []
        for k in range(count):
            at = pl.multiple_of((first + k) * LANES, LANES)
            parts += [table_ref[:, pl.ds(at, LANES)], pad]
        if count < PACK:
            parts.append(jnp.zeros(((PACK - count) * FPAD, LANES), BF16))
        packed = jnp.concatenate(parts, axis=0).T.astype(F32)
        for k in range(count):
            at = pl.multiple_of((first + k) * LANES, LANES)
            turned[pl.ds(at, LANES), :] = jnp.where(slot == k, packed, 0.0)

    def turn_units(i, _):
        for u in range(4):
            turn((i * 4 + u) * PACK, PACK)
        return 0

    blocks = entries // LANES
    loops = blocks // (4 * PACK)
    lax.fori_loop(0, loops, turn_units, 0)
    for first in range(loops * 4 * PACK, blocks, PACK):
        turn(first, min(PACK, blocks - first))

    place = (iota((LANES, LANES), 1) - shift_ref[0]) & (LANES - 1)
    row = iota((LANES, LANES), 0)
    move = (row % FPAD == place % FPAD) & (place // FPAD % 2 == group)
    move = jnp.where(move, 1.0, 0.0).astype(BF16)
    place = (iota((rows // 2, LANES), 1) - shift_ref[0]) & (LANES - 1)

    def look(i, _):
        def find(j, _):
            o = i * batch + j
            base = spot_ref[o // (LANES // per)] + o % (LANES // per) * per
            to = pl.multiple_of(j * rows, rows)
            for t in range(STEPS):
                for s in range(per):
                    at = id_ref[base + ((group * STEPS + t) * LANES + s)]
                    found[pl.ds(to + (t * per + s), 1), :] = turned[pl.ds(at, 1), :]
            return 0

        lax.fori_loop(0, batch, find, 0)
        moved = jnp.dot(found[...].astype(BF16), move, preferred_element_type=F32)
        for j in range(batch):
            a = moved[j * rows : j * rows + rows // 2]
            b = moved[j * rows + rows // 2 : (j + 1) * rows]
            both = jnp.where(place < 2 * FPAD, a, b)
            if other_ref is not None:
                both = both + other_ref[i * batch + j].astype(F32)
            out_ref[i * batch + j] = both.astype(BF16)
        return 0

    lax.fori_loop(0, owners // batch, look, 0)


def look_up(ids, group, spots, table, shift, owners, *other):
    groups, _, streams = ids.shape
    rows = streams * STEPS // owners
    vmem = pl.BlockSpec(memory_space=pltpu.VMEM)
    smem = pl.BlockSpec(memory_space=pltpu.SMEM)
    return pl.pallas_call(
        functools.partial(look_kernel, group=group),
        in_specs=[smem, smem, smem, vmem] + [vmem] * len(other),
        out_specs=vmem,
        out_shape=jax.ShapeDtypeStruct((groups * owners, rows // 2, LANES), BF16),
        scratch_shapes=[
            pltpu.VMEM((table.shape[1], LANES), F32),
            pltpu.VMEM((32 * rows, LANES), F32),
        ],
        compiler_params=pltpu.CompilerParams(vmem_limit_bytes=(table.shape[1] // 2048 + 14) * MIB),
        cost_estimate=pl.CostEstimate(
            flops=0, bytes_accessed=(20 + table.shape[1] // 3000) * MIB, transcendentals=0
        ),
        name="look_up",
    )(shift, spots, ids.reshape(-1), table, *other)


def collect_rows_kernel(order_ref, spot_ref, *refs, owners):
    a_refs = refs[:owners]
    res_ref, a_all, res_all, done, a_sem, res_sem = refs[owners:]
    rows, depth = a_refs[0].shape
    size = rows // owners
    copies = []
    for b in range(owners):
        to = pl.ds(pl.multiple_of(spot_ref[b] * size, size), size)
        for k in range(owners):
            at = pl.multiple_of(order_ref[k] * depth, depth)
            source = a_refs[k].at[b * size : (b + 1) * size]
            target = a_all.at[to, pl.ds(at, depth)]
            copies.append(pltpu.make_async_copy(source, target, a_sem.at[b, k]))
        for t in range(STEPS):
            target = res_all.at[spot_ref[b], t]
            copies.append(pltpu.make_async_copy(res_ref.at[t, b], target, res_sem.at[b, t]))
    for copy in copies:
        copy.start()
    for copy in copies:
        copy.wait()
    done[...] = jnp.zeros_like(done)


def collect_rows(attended, order, spots, residual):
    owners = len(attended)
    rows, depth = attended[0].shape
    width = residual.shape[-1]
    vmem = pl.BlockSpec(memory_space=pltpu.VMEM)
    smem = pl.BlockSpec(memory_space=pltpu.SMEM)
    return pl.pallas_call(
        functools.partial(collect_rows_kernel, owners=owners),
        in_specs=[smem, smem] + [pl.BlockSpec(memory_space=pl.ANY)] * (owners + 1),
        out_specs=[vmem] * 3,
        out_shape=[
            jax.ShapeDtypeStruct((rows, owners * depth), BF16),
            jax.ShapeDtypeStruct((owners, STEPS, rows // STEPS // owners, width), BF16),
            jax.ShapeDtypeStruct((8, LANES), F32),
        ],
        scratch_shapes=[pltpu.SemaphoreType.DMA((owners, n)) for n in (owners, STEPS)],
        compiler_params=pltpu.CompilerParams(vmem_limit_bytes=12 * MIB),
        cost_estimate=pl.CostEstimate(flops=0, bytes_accessed=8 * MIB, transcendentals=0),
        name="collect_rows",
    )(order, spots, *attended, residual)


def restore_kernel(spot_ref, x_ref, out_ref, sems):
    steps, owners = out_ref.shape[:2]
    copies = [
        pltpu.make_async_copy(x_ref.at[spot_ref[b], t], out_ref.at[t, b], sems.at[b, t])
        for b in range(owners)
        for t in range(steps)
    ]
    for copy in copies:
        copy.start()
    for copy in copies:
        copy.wait()


def restore(x, spots):
    owners, steps, per, width = x.shape
    anywhere = pl.BlockSpec(memory_space=pl.ANY)
    return pl.pallas_call(
        restore_kernel,
        in_specs=[pl.BlockSpec(memory_space=pltpu.SMEM), anywhere],
        out_specs=anywhere,
        out_shape=jax.ShapeDtypeStruct((steps, owners, per, width), x.dtype),
        scratch_shapes=[pltpu.SemaphoreType.DMA((owners, steps))],
        compiler_params=pltpu.CompilerParams(vmem_limit_bytes=12 * MIB),
        cost_estimate=pl.CostEstimate(flops=0, bytes_accessed=2 * MIB, transcendentals=0),
        name="restore",
    )(spots, x)


def collect_weight_kernel(subs_ref, done_ref, *refs):
    del done_ref
    *w_refs, w_all, sems = refs
    copies = []
    for w_ref in w_refs:
        for k in range(w_ref.shape[1]):
            sub = len(copies)
            copies.append(
                pltpu.make_async_copy(w_ref.at[:, k], w_all.at[:, subs_ref[sub]], sems.at[sub])
            )
    for copy in copies:
        copy.start()
    for copy in copies:
        copy.wait()


def collect_weight(weights, subs, done):
    owners, _, size, width = weights[0].shape
    parts = subs.shape[0]
    return pl.pallas_call(
        collect_weight_kernel,
        in_specs=[pl.BlockSpec(memory_space=pltpu.SMEM)]
        + [pl.BlockSpec(memory_space=pl.ANY)] * (len(weights) + 1),
        out_specs=pl.BlockSpec(memory_space=pltpu.VMEM),
        out_shape=jax.ShapeDtypeStruct((owners, parts, size, width), BF16),
        scratch_shapes=[pltpu.SemaphoreType.DMA((parts,))],
        compiler_params=pltpu.CompilerParams(vmem_limit_bytes=12 * MIB),
        cost_estimate=pl.CostEstimate(flops=0, bytes_accessed=10 * MIB, transcendentals=0),
        name="collect_weight",
    )(subs, done, *weights)


def place_kernel(emb_ref, out_ref, *, feats):
    holders, half, _ = emb_ref.shape
    lane = iota((half, LANES), 1)
    for tile in range(holders * feats // LANES):
        start = tile * LANES
        found = [jnp.zeros((half, LANES), F32) for _ in range(PACK)]
        for h in range(start // feats, min((start + LANES - 1) // feats, holders - 1) + 1):
            row = emb_ref[h].astype(F32)
            low, high = max(h * feats - start, 0), min((h + 1) * feats - start, LANES)
            for g in range(PACK):
                spot = (lane - g * FPAD) & (LANES - 1)
                found[g] = jnp.where((spot >= low) & (spot < high), row, found[g])
        a = found[0] + pltpu.roll(found[1], LANES - FPAD, 1)
        b = found[2] + pltpu.roll(found[3], LANES - FPAD, 1)
        b = pltpu.roll(b, LANES // 2, 1)
        out_ref[:half, start : start + LANES] = a
        out_ref[half:, start : start + LANES] = b


def place(emb, talk):
    holders, half, _ = emb.shape
    blocks = 4
    return pl.pallas_call(
        functools.partial(place_kernel, feats=talk // holders),
        grid=(blocks,),
        in_specs=[pl.BlockSpec((holders // blocks, half, LANES), lambda i: (i, 0, 0))],
        out_specs=pl.BlockSpec((2 * half, talk // blocks), lambda i: (0, i)),
        out_shape=jax.ShapeDtypeStruct((2 * half, talk), F32),
        compiler_params=pltpu.CompilerParams(vmem_limit_bytes=8 * MIB),
        cost_estimate=pl.CostEstimate(flops=0, bytes_accessed=8 * MIB, transcendentals=0),
        name="place",
    )(emb)


def finish_kernel(*refs):
    *part_refs, emb_ref, gain_ref, out_ref, mixed = refs
    rows, talk = out_ref.shape
    halves = [part_refs[: len(part_refs) // 2], part_refs[len(part_refs) // 2 :]]
    square = jnp.zeros((rows, LANES), F32)
    for c in range(talk // LANES):
        cols = slice(c * LANES, (c + 1) * LANES)
        half, at = divmod(c * LANES, talk // 2)
        total = emb_ref[:, cols]
        for ref in halves[half]:
            total = total + ref[:rows, at : at + LANES].astype(F32)
        mixed[:, cols] = total
        square = square + total * total
    mean = jnp.sum(square, axis=-1, keepdims=True) * (1.0 / talk)
    factor = lax.rsqrt(mean + 1e-06)
    for c in range(talk // LANES):
        cols = slice(c * LANES, (c + 1) * LANES)
        gain = gain_ref[:, cols].astype(F32)
        out_ref[:, cols] = (mixed[:, cols] * factor * gain).astype(BF16)


def finish(parts, emb, gain):
    rows, talk = emb.shape
    vmem = pl.BlockSpec(memory_space=pltpu.VMEM)
    return pl.pallas_call(
        finish_kernel,
        in_specs=[vmem] * (len(parts) + 2),
        out_specs=vmem,
        out_shape=jax.ShapeDtypeStruct((rows, talk), BF16),
        scratch_shapes=[pltpu.VMEM((rows, talk), F32)],
        compiler_params=pltpu.CompilerParams(vmem_limit_bytes=8 * MIB),
        cost_estimate=pl.CostEstimate(flops=0, bytes_accessed=8 * MIB, transcendentals=0),
        name="finish",
    )(*parts, emb, gain)


def bridge_parts(hidden, bridge_weight):
    up, down, _, across = tensor_pairs()
    talk = bridge_weight.shape[1]
    rows = hidden.shape[0] // 4
    own = rows // 2

    def product(block, half):
        weight = bridge_weight[:, half * (talk // 2) : (half + 1) * (talk // 2)]
        block = hidden[block * rows : (block + 1) * rows]
        return jnp.dot(block, weight, preferred_element_type=F32)

    by_up = send(product(2, 0).astype(BF16), up)
    by_down = send(product(2, 1).astype(BF16), down)
    from_down = [send(product(3, 0).astype(BF16), down)]
    from_up = [None, send(product(1, 1).astype(BF16), up)]
    from_up[0] = send((product(1, 0) + by_up.astype(F32)).astype(BF16), up)
    from_down.append(send((product(3, 1) + by_down.astype(F32)).astype(BF16), down))
    parts = []
    for half in range(2):
        mine = product(0, half)
        other = mine[own:] + from_up[half][own:].astype(F32) + from_down[half][own:].astype(F32)
        parts += [mine, from_up[half], from_down[half], send(other.astype(BF16), across)]
    return parts


def gather_ids(ids, share, later):
    count = lax.axis_size("dp")
    size = ids.size
    get = lambda x, peer: lax.ppermute(x, "dp", [(peer(i), i) for i in range(count)])
    turn = lambda by: lambda i: i // 8 * 8 + (i + 2 * by) % 8
    across_y, share = lax.optimization_barrier((get(ids, lambda i: i ^ 8), share))
    ids = jnp.stack([ids, across_y])
    ids = jnp.concatenate([ids, get(ids, lambda i: i ^ 1)])
    ids, later = lax.optimization_barrier((ids, later))
    ids = jnp.concatenate([ids] + [get(ids, turn(by)) for by in (1, 2, 3)])
    me = lax.axis_index("dp")
    peer = jnp.arange(count, dtype=jnp.int32)
    across = (peer // 2 - me // 2) % 4
    other = (peer % 2 != me % 2) * 2 + (peer // 8 != me // 8)
    return share, later, ids, ((across * 4 + other) * size).astype(jnp.int32)


def tensor_pairs():
    size = lax.axis_size("tensor")
    along = lambda by: [(i, (i + 2 * by) % size) for i in range(size)]
    return along(1), along(-1), along(2), [(i, i ^ 1) for i in range(size)]


def send(x, pairs):
    return lax.ppermute(x, "tensor", pairs)


def gather_first(own):
    return [send(own, pairs) for pairs in tensor_pairs()]


def gather_second(first):
    up, down, _, across = tensor_pairs()
    _, _, far, beside = first
    return [send(beside, up), send(beside, down), send(far, across)]


def peers_order():
    size = lax.axis_size("tensor")
    me = lax.axis_index("tensor")
    x, y = me // 2, me % 2
    spot = lambda k, other: (x + k) % (size // 2) * 2 + (y + other) % 2
    order = [(0, 0), (3, 0), (1, 0), (2, 0), (0, 1), (3, 1), (1, 1), (2, 1)]
    order = jnp.stack([spot(*o) for o in order]).astype(jnp.int32)
    peer = jnp.arange(size, dtype=jnp.int32)
    return order, (peer // 2 - x) % (size // 2) * 2 + (peer % 2 != y)


def share_kernel(subs_ref, w_ref, out_ref, sems):
    owners, parts, size, width = out_ref.shape
    copies = []
    for k in range(parts):
        rows = pl.ds(pl.multiple_of(subs_ref[k] * size, size), size)
        for t in range(owners):
            copies.append(
                pltpu.make_async_copy(
                    w_ref.at[rows, t * width : (t + 1) * width], out_ref.at[t, k], sems.at[t, k]
                )
            )
    for copy in copies:
        copy.start()
    for copy in copies:
        copy.wait()


def share_rows(out_weight, subs, size, width):
    owners = out_weight.shape[1] // width
    return pl.pallas_call(
        share_kernel,
        in_specs=[pl.BlockSpec(memory_space=pltpu.SMEM), pl.BlockSpec(memory_space=pltpu.HBM)],
        out_specs=pl.BlockSpec(memory_space=pltpu.VMEM),
        out_shape=jax.ShapeDtypeStruct((owners, subs.shape[0], size, width), BF16),
        scratch_shapes=[pltpu.SemaphoreType.DMA((owners, subs.shape[0]))],
        compiler_params=pltpu.CompilerParams(vmem_limit_bytes=58 * MIB),
        cost_estimate=pl.CostEstimate(flops=0, bytes_accessed=4 * MIB, transcendentals=0),
        name="share_rows",
    )(subs, out_weight)


def weight_first(out_weight, width):
    depth = out_weight.shape[0]
    tensor = out_weight.shape[1] // width
    size = depth // 8
    me = lax.axis_index("dp")
    core, odd = me % 2, me // 2 % 2
    sub_a, sub_b = core * 4 + odd, core * 4 + 3 - odd
    pair = jnp.stack([sub_a, sub_b]).astype(jnp.int32)
    share = share_rows(out_weight, pair, size, width)

    own = [sub_a, sub_b, core * 4 + 1 - odd, core * 4 + 2 + odd]
    return share, jnp.stack(own + [(k + 4) % 8 for k in own]).astype(jnp.int32)


def weight_second(share):
    count = lax.axis_size("dp")
    turn = lambda i, by: i // 8 * 8 + (i + 2 * by) % 8
    z_of = lambda i: i // 2 % 4
    pairs_a = [(i, turn(i, -1 if z_of(i) % 2 else 1)) for i in range(count)]
    pairs_b = [(i, turn(i, 1 if z_of(i) % 2 else -1)) for i in range(count)]
    beside_a = lax.ppermute(share[:, :1], "dp", pairs_a)
    beside_b = lax.ppermute(share[:, 1:], "dp", pairs_b)
    return [share, beside_a, beside_b]


def weight_third(weights):
    cores = [(i, i ^ 1) for i in range(lax.axis_size("dp"))]
    return weights + [lax.ppermute(x, "dp", cores) for x in weights]


def local(
    query,
    new_keys,
    new_values,
    cache_keys,
    cache_values,
    cache_lengths,
    residual,
    out_weight,
    bridge_weight,
    text_table,
    codec_table,
    tokens,
    frames,
    talk_gain,
):
    steps, streams, depth = query.shape
    width = residual.shape[2]
    talk = bridge_weight.shape[1]
    tensor = out_weight.shape[1] // width
    dp = lax.axis_size("dp")
    rows = steps * streams
    per = streams // tensor

    feats = text_table.shape[0]
    shift = (lax.axis_index("dp") * tensor + lax.axis_index("tensor")) * feats % LANES
    shift = shift[None].astype(jnp.int32)
    share, subs = weight_first(out_weight, width)
    ids = jnp.concatenate([tokens, frames], axis=0)
    share, query, ids, spots = gather_ids(ids, share, query)
    share = lax.all_to_all(share, "tensor", 0, 0, tiled=True)

    attended = attention(query, new_keys, new_values, cache_keys, cache_values, cache_lengths)
    attended, ids = lax.optimization_barrier((attended.reshape(rows, depth), ids))
    first = gather_first(attended)
    text = look_up(ids, 0, spots, text_table, shift, tensor)
    first, text, share = lax.optimization_barrier((first, text, share))
    weights = weight_second(share)
    attended = [attended] + first + gather_second(first)
    emb = look_up(ids, 1, spots, codec_table, shift, tensor, text)
    residual = residual.reshape(steps, tensor, per, width)
    order, owner_spots = peers_order()
    attended, mine, done = collect_rows(attended, order, owner_spots, residual)
    weights, done, emb = lax.optimization_barrier((weights, done, emb))
    emb = lax.all_to_all(emb, BOTH, 0, 0, tiled=True)
    weight = collect_weight(weight_third(weights), subs, done)
    hidden = jnp.dot(attended, weight.reshape(tensor * depth, width), preferred_element_type=F32)
    hidden = (mine.reshape(rows, width).astype(F32) + hidden).astype(BF16)
    parts = bridge_parts(hidden, bridge_weight)
    talker = finish(parts, place(emb, talk), talk_gain.reshape(1, talk))
    hidden = restore(hidden.reshape(tensor, steps, per, width), owner_spots)
    return hidden.reshape(steps, streams, width), talker.reshape(steps, per, talk)


def solution(mesh):
    in_specs = (
        P(None, "dp", "tensor"),
        P(None, "dp", "tensor"),
        P(None, "dp", "tensor"),
        P("dp", None, "tensor"),
        P("dp", None, "tensor"),
        P("dp"),
        P(None, "dp", "tensor"),
        P("tensor", None),
        P("tensor", None),
        P(("dp", "tensor"), None),
        P(("dp", "tensor"), None),
        P(None, "dp"),
        P(None, "dp"),
        P(),
    )
    out_specs = (P(None, "dp", "tensor"), P(None, ("dp", "tensor"), None))
    return jax.shard_map(local, mesh=mesh, in_specs=in_specs, out_specs=out_specs, check_vma=False)
```

```python
import functools

import jax
import jax.numpy as jnp
from jax import lax
from jax.experimental import pallas as pl
from jax.experimental.pallas import tpu as pltpu
from jax.sharding import PartitionSpec as P

QH = 32
KVH = 8
HD = 128
CAP = 64
GROUP = QH // KVH
STEPS = 4
SB = 16
BLOCKS = 2
LANES = 128
FPAD = 32
PACK = LANES // FPAD
UNITS = 8
BF16 = jnp.bfloat16
F32 = jnp.float32
BOTH = ("dp", "tensor")
MIB = 1 << 20


def iota(shape, dim):
    return lax.broadcasted_iota(jnp.int32, shape, dim)


def attention_kernel(len_ref, q_ref, ck_ref, cv_ref, nk_ref, nv_ref, out_ref):
    some = SB // 2
    rows = STEPS * GROUP * some
    scale = 1.0 / HD**0.5
    contract = (((1,), (1,)), ((), ()))
    query = [
        q_ref[t, :, h * HD : (h + 1) * HD].astype(F32) for t in range(STEPS) for h in range(GROUP)
    ]
    fresh = [[ref[t].astype(F32) for t in range(STEPS)] for ref in (nk_ref, nv_ref)]
    own = iota((rows, 1), 0) % some
    start = own * CAP
    spot = iota((rows, some * CAP), 1)
    row, col = iota((rows, STEPS * some), 0), iota((rows, STEPS * some), 1)
    seen = (row % some == col % some) & (col // some <= row // (GROUP * some))
    results = []
    for part in range(2 * BLOCKS):
        here = slice(part * some, (part + 1) * some)
        queries = jnp.concatenate([q[here] for q in query], axis=0).astype(BF16)
        cached_k = ck_ref[here].reshape(some * CAP, HD)
        cached_v = cv_ref[here].reshape(some * CAP, HD)
        fresh_k, fresh_v = [jnp.concatenate([x[here] for x in f], axis=0).astype(BF16) for f in fresh]
        score_c = lax.dot_general(queries, cached_k, contract, preferred_element_type=F32) * scale
        score_n = lax.dot_general(queries, fresh_k, contract, preferred_element_type=F32) * scale
        stop = start + jnp.concatenate([len_ref[here, :1]] * (STEPS * GROUP), axis=0)
        score_c = jnp.where((spot >= start) & (spot < stop), score_c, -1e30)
        score_n = jnp.where(seen, score_n, -1e30)
        top = jnp.maximum(
            jnp.max(score_c, axis=-1, keepdims=True), jnp.max(score_n, axis=-1, keepdims=True)
        )
        exp_c = jnp.exp(score_c - top)
        exp_n = jnp.exp(score_n - top)
        total = jnp.sum(exp_c, axis=-1, keepdims=True) + jnp.sum(exp_n, axis=-1, keepdims=True)
        inverse = 1.0 / total
        weight_c = (exp_c * inverse).astype(BF16)
        weight_n = (exp_n * inverse).astype(BF16)
        attended = jnp.dot(weight_c, cached_v, preferred_element_type=F32)
        results.append(attended + jnp.dot(weight_n, fresh_v, preferred_element_type=F32))
    for t in range(STEPS):
        for h in range(GROUP):
            at = (t * GROUP + h) * some
            for b in range(BLOCKS):
                both = [r[at : at + some] for r in results[2 * b : 2 * b + 2]]
                both = jnp.concatenate(both, axis=0).astype(BF16)
                out_ref[b, t, :, h * HD : (h + 1) * HD] = both


def attention(query, new_keys, new_values, cache_keys, cache_values, cache_lengths):
    steps, streams, width = query.shape
    blocks = streams // SB
    lengths = jnp.broadcast_to(cache_lengths[:, None], (streams, LANES))
    fresh = pl.BlockSpec((steps, BLOCKS * SB, HD), lambda i: (0, i, 0))
    cached = pl.BlockSpec((BLOCKS * SB, CAP, HD), lambda i: (i, 0, 0))
    return pl.pallas_call(
        attention_kernel,
        grid=(blocks // BLOCKS,),
        in_specs=[
            pl.BlockSpec((BLOCKS * SB, LANES), lambda i: (i, 0)),
            pl.BlockSpec((steps, BLOCKS * SB, width), lambda i: (0, i, 0)),
            cached,
            cached,
            fresh,
            fresh,
        ],
        out_specs=pl.BlockSpec((BLOCKS, steps, SB, width), lambda i: (i, 0, 0, 0)),
        out_shape=jax.ShapeDtypeStruct((blocks, steps, SB, width), BF16),
        compiler_params=pltpu.CompilerParams(vmem_limit_bytes=58 * MIB),
        cost_estimate=pl.CostEstimate(flops=8 * 10**9, bytes_accessed=6 * MIB, transcendentals=0),
        name="attention",
    )(lengths, query, cache_keys, cache_values, new_keys, new_values)


def look_kernel(shift_ref, spot_ref, id_ref, table_ref, *refs, group):
    other_ref = refs[0] if len(refs) == 4 else None
    out_ref, turned, found = refs[-3:]
    feats, entries = table_ref.shape
    owners = out_ref.shape[0]
    rows = 2 * out_ref.shape[1]
    per = rows // STEPS
    batch = found.shape[0] // rows
    pad = jnp.zeros((FPAD - feats, LANES), BF16)
    slot = iota((LANES, LANES), 1) // FPAD

    def turn(first, count):
        parts = []
        for k in range(count):
            at = pl.multiple_of((first + k) * LANES, LANES)
            parts += [table_ref[:, pl.ds(at, LANES)], pad]
        if count < PACK:
            parts.append(jnp.zeros(((PACK - count) * FPAD, LANES), BF16))
        packed = jnp.concatenate(parts, axis=0).T.astype(F32)
        for k in range(count):
            at = pl.multiple_of((first + k) * LANES, LANES)
            turned[pl.ds(at, LANES), :] = jnp.where(slot == k, packed, 0.0)

    def turn_units(i, _):
        for u in range(UNITS):
            turn((i * UNITS + u) * PACK, PACK)
        return 0

    blocks = entries // LANES
    loops = blocks // (UNITS * PACK)
    lax.fori_loop(0, loops, turn_units, 0)
    for first in range(loops * UNITS * PACK, blocks, PACK):
        turn(first, min(PACK, blocks - first))

    place = (iota((LANES, LANES), 1) - shift_ref[0]) & (LANES - 1)
    row = iota((LANES, LANES), 0)
    move = (row % FPAD == place % FPAD) & (place // FPAD % 2 == group)
    move = jnp.where(move, 1.0, 0.0).astype(BF16)
    place = (iota((rows // 2, LANES), 1) - shift_ref[0]) & (LANES - 1)

    def look(i, _):
        def find(j, _):
            o = i * batch + j
            base = spot_ref[o // (LANES // per)] + o % (LANES // per) * per
            to = pl.multiple_of(j * rows, rows)
            for t in range(STEPS):
                for s in range(per):
                    at = id_ref[base + ((group * STEPS + t) * LANES + s)]
                    found[pl.ds(to + (t * per + s), 1), :] = turned[pl.ds(at, 1), :]
            return 0

        lax.fori_loop(0, batch, find, 0, unroll=4)
        moved = jnp.dot(found[...].astype(BF16), move, preferred_element_type=F32)
        for j in range(batch):
            a = moved[j * rows : j * rows + rows // 2]
            b = moved[j * rows + rows // 2 : (j + 1) * rows]
            both = jnp.where(place < 2 * FPAD, a, b)
            if other_ref is not None:
                both = both + other_ref[i * batch + j].astype(F32)
            out_ref[i * batch + j] = both.astype(BF16)
        return 0

    lax.fori_loop(0, owners // batch, look, 0)


def look_up(ids, group, spots, table, shift, owners, *other):
    groups, _, streams = ids.shape
    rows = streams * STEPS // owners
    vmem = pl.BlockSpec(memory_space=pltpu.VMEM)
    smem = pl.BlockSpec(memory_space=pltpu.SMEM)
    return pl.pallas_call(
        functools.partial(look_kernel, group=group),
        in_specs=[smem, smem, smem, vmem] + [vmem] * len(other),
        out_specs=vmem,
        out_shape=jax.ShapeDtypeStruct((groups * owners, rows // 2, LANES), BF16),
        scratch_shapes=[
            pltpu.VMEM((table.shape[1], LANES), F32),
            pltpu.VMEM((32 * rows, LANES), F32),
        ],
        compiler_params=pltpu.CompilerParams(vmem_limit_bytes=(table.shape[1] // 2048 + 14) * MIB),
        cost_estimate=pl.CostEstimate(
            flops=0, bytes_accessed=table.shape[1] // 1000 * MIB, transcendentals=0
        ),
        name="look_up",
    )(shift, spots, ids.reshape(-1), table, *other)


def collect_rows_kernel(order_ref, spot_ref, *refs, owners):
    a_refs = refs[:owners]
    res_ref, a_all, res_all, done, a_sem, res_sem = refs[owners:]
    rows, depth = a_refs[0].shape
    size = rows // owners
    copies = []
    for b in range(owners):
        to = pl.ds(pl.multiple_of(spot_ref[b] * size, size), size)
        for k in range(owners):
            at = pl.multiple_of(order_ref[k] * depth, depth)
            source = a_refs[k].at[b * size : (b + 1) * size]
            target = a_all.at[to, pl.ds(at, depth)]
            copies.append(pltpu.make_async_copy(source, target, a_sem.at[b, k]))
        for t in range(STEPS):
            target = res_all.at[spot_ref[b], t]
            copies.append(pltpu.make_async_copy(res_ref.at[t, b], target, res_sem.at[b, t]))
    for copy in copies:
        copy.start()
    for copy in copies:
        copy.wait()
    done[...] = jnp.zeros_like(done)


def collect_rows(attended, order, spots, residual):
    owners = len(attended)
    rows, depth = attended[0].shape
    width = residual.shape[-1]
    vmem = pl.BlockSpec(memory_space=pltpu.VMEM)
    smem = pl.BlockSpec(memory_space=pltpu.SMEM)
    return pl.pallas_call(
        functools.partial(collect_rows_kernel, owners=owners),
        in_specs=[smem, smem] + [pl.BlockSpec(memory_space=pl.ANY)] * (owners + 1),
        out_specs=[vmem] * 3,
        out_shape=[
            jax.ShapeDtypeStruct((rows, owners * depth), BF16),
            jax.ShapeDtypeStruct((owners, STEPS, rows // STEPS // owners, width), BF16),
            jax.ShapeDtypeStruct((8, LANES), F32),
        ],
        scratch_shapes=[pltpu.SemaphoreType.DMA((owners, n)) for n in (owners, STEPS)],
        compiler_params=pltpu.CompilerParams(vmem_limit_bytes=58 * MIB),
        cost_estimate=pl.CostEstimate(flops=0, bytes_accessed=8 * MIB, transcendentals=0),
        name="collect_rows",
    )(order, spots, *attended, residual)


def restore_kernel(spot_ref, x_ref, out_ref, sems):
    steps, owners = out_ref.shape[:2]
    copies = [
        pltpu.make_async_copy(x_ref.at[spot_ref[b], t], out_ref.at[t, b], sems.at[b, t])
        for b in range(owners)
        for t in range(steps)
    ]
    for copy in copies:
        copy.start()
    for copy in copies:
        copy.wait()


def restore(x, spots):
    owners, steps, per, width = x.shape
    anywhere = pl.BlockSpec(memory_space=pl.ANY)
    return pl.pallas_call(
        restore_kernel,
        in_specs=[pl.BlockSpec(memory_space=pltpu.SMEM), anywhere],
        out_specs=anywhere,
        out_shape=jax.ShapeDtypeStruct((steps, owners, per, width), x.dtype),
        scratch_shapes=[pltpu.SemaphoreType.DMA((owners, steps))],
        compiler_params=pltpu.CompilerParams(vmem_limit_bytes=12 * MIB),
        cost_estimate=pl.CostEstimate(flops=0, bytes_accessed=2 * MIB, transcendentals=0),
        name="restore",
    )(spots, x)


def collect_weight_kernel(subs_ref, done_ref, *refs):
    del done_ref
    *w_refs, w_all, sems = refs
    copies = []
    for w_ref in w_refs:
        for k in range(w_ref.shape[1]):
            sub = len(copies)
            copies.append(
                pltpu.make_async_copy(w_ref.at[:, k], w_all.at[:, subs_ref[sub]], sems.at[sub])
            )
    for copy in copies:
        copy.start()
    for copy in copies:
        copy.wait()


def collect_weight(weights, subs, done):
    owners, _, size, width = weights[0].shape
    parts = subs.shape[0]
    return pl.pallas_call(
        collect_weight_kernel,
        in_specs=[pl.BlockSpec(memory_space=pltpu.SMEM)]
        + [pl.BlockSpec(memory_space=pl.ANY)] * (len(weights) + 1),
        out_specs=pl.BlockSpec(memory_space=pltpu.VMEM),
        out_shape=jax.ShapeDtypeStruct((owners, parts, size, width), BF16),
        scratch_shapes=[pltpu.SemaphoreType.DMA((parts,))],
        compiler_params=pltpu.CompilerParams(vmem_limit_bytes=12 * MIB),
        cost_estimate=pl.CostEstimate(flops=0, bytes_accessed=10 * MIB, transcendentals=0),
        name="collect_weight",
    )(subs, done, *weights)


def place_kernel(emb_ref, out_ref, *, feats):
    holders, half, _ = emb_ref.shape
    lane = iota((half, LANES), 1)
    for tile in range(holders * feats // LANES):
        start = tile * LANES
        found = [jnp.zeros((half, LANES), F32) for _ in range(PACK)]
        for h in range(start // feats, min((start + LANES - 1) // feats, holders - 1) + 1):
            row = emb_ref[h].astype(F32)
            low, high = max(h * feats - start, 0), min((h + 1) * feats - start, LANES)
            for g in range(PACK):
                spot = (lane - g * FPAD) & (LANES - 1)
                found[g] = jnp.where((spot >= low) & (spot < high), row, found[g])
        a = found[0] + pltpu.roll(found[1], LANES - FPAD, 1)
        b = found[2] + pltpu.roll(found[3], LANES - FPAD, 1)
        b = pltpu.roll(b, LANES // 2, 1)
        out_ref[:half, start : start + LANES] = a
        out_ref[half:, start : start + LANES] = b


def place(emb, talk):
    holders, half, _ = emb.shape
    blocks = 4
    return pl.pallas_call(
        functools.partial(place_kernel, feats=talk // holders),
        grid=(blocks,),
        in_specs=[pl.BlockSpec((holders // blocks, half, LANES), lambda i: (i, 0, 0))],
        out_specs=pl.BlockSpec((2 * half, talk // blocks), lambda i: (0, i)),
        out_shape=jax.ShapeDtypeStruct((2 * half, talk), F32),
        compiler_params=pltpu.CompilerParams(vmem_limit_bytes=8 * MIB),
        cost_estimate=pl.CostEstimate(flops=0, bytes_accessed=8 * MIB, transcendentals=0),
        name="place",
    )(emb)


def finish_kernel(*refs):
    *part_refs, emb_ref, gain_ref, out_ref, mixed = refs
    rows, talk = out_ref.shape
    halves = [part_refs[: len(part_refs) // 2], part_refs[len(part_refs) // 2 :]]
    square = jnp.zeros((rows, LANES), F32)
    for c in range(talk // LANES):
        cols = slice(c * LANES, (c + 1) * LANES)
        half, at = divmod(c * LANES, talk // 2)
        total = emb_ref[:, cols]
        for ref in halves[half]:
            total = total + ref[:rows, at : at + LANES].astype(F32)
        mixed[:, cols] = total
        square = square + total * total
    mean = jnp.sum(square, axis=-1, keepdims=True) * (1.0 / talk)
    factor = lax.rsqrt(mean + 1e-06)
    for c in range(talk // LANES):
        cols = slice(c * LANES, (c + 1) * LANES)
        gain = gain_ref[:, cols].astype(F32)
        out_ref[:, cols] = (mixed[:, cols] * factor * gain).astype(BF16)


def finish(parts, emb, gain):
    rows, talk = emb.shape
    vmem = pl.BlockSpec(memory_space=pltpu.VMEM)
    return pl.pallas_call(
        finish_kernel,
        in_specs=[vmem] * (len(parts) + 2),
        out_specs=vmem,
        out_shape=jax.ShapeDtypeStruct((rows, talk), BF16),
        scratch_shapes=[pltpu.VMEM((rows, talk), F32)],
        compiler_params=pltpu.CompilerParams(vmem_limit_bytes=8 * MIB),
        cost_estimate=pl.CostEstimate(flops=0, bytes_accessed=8 * MIB, transcendentals=0),
        name="finish",
    )(*parts, emb, gain)


def bridge_parts(hidden, bridge_weight):
    up, down, _, across = tensor_pairs()
    talk = bridge_weight.shape[1]
    rows = hidden.shape[0] // 4
    own = rows // 2

    def product(block, half):
        weight = bridge_weight[:, half * (talk // 2) : (half + 1) * (talk // 2)]
        block = hidden[block * rows : (block + 1) * rows]
        return jnp.dot(block, weight, preferred_element_type=F32)

    by_up = send(product(2, 0).astype(BF16), up)
    by_down = send(product(2, 1).astype(BF16), down)
    from_down = [send(product(3, 0).astype(BF16), down)]
    from_up = [None, send(product(1, 1).astype(BF16), up)]
    from_up[0] = send((product(1, 0) + by_up.astype(F32)).astype(BF16), up)
    from_down.append(send((product(3, 1) + by_down.astype(F32)).astype(BF16), down))
    parts = []
    for half in range(2):
        mine = product(0, half)
        other = mine[own:] + from_up[half][own:].astype(F32) + from_down[half][own:].astype(F32)
        parts += [mine, from_up[half], from_down[half], send(other.astype(BF16), across)]
    return parts


def gather_ids(ids, share, later):
    count = lax.axis_size("dp")
    size = ids.size
    get = lambda x, peer: lax.ppermute(x, "dp", [(peer(i), i) for i in range(count)])
    turn = lambda by: lambda i: i // 8 * 8 + (i + 2 * by) % 8
    across_y, share = lax.optimization_barrier((get(ids, lambda i: i ^ 8), share))
    ids = jnp.stack([ids, across_y])
    ids = jnp.concatenate([ids, get(ids, lambda i: i ^ 1)])
    ids, later = lax.optimization_barrier((ids, later))
    ids = jnp.concatenate([ids] + [get(ids, turn(by)) for by in (1, 2, 3)])
    me = lax.axis_index("dp")
    peer = jnp.arange(count, dtype=jnp.int32)
    across = (peer // 2 - me // 2) % 4
    other = (peer % 2 != me % 2) * 2 + (peer // 8 != me // 8)
    return share, later, ids, ((across * 4 + other) * size).astype(jnp.int32)


def tensor_pairs():
    size = lax.axis_size("tensor")
    along = lambda by: [(i, (i + 2 * by) % size) for i in range(size)]
    return along(1), along(-1), along(2), [(i, i ^ 1) for i in range(size)]


def send(x, pairs):
    return lax.ppermute(x, "tensor", pairs)


def gather_first(own):
    return [send(own, pairs) for pairs in tensor_pairs()]


def gather_second(first):
    up, down, _, across = tensor_pairs()
    _, _, far, beside = first
    return [send(beside, up), send(beside, down), send(far, across)]


def peers_order():
    size = lax.axis_size("tensor")
    me = lax.axis_index("tensor")
    x, y = me // 2, me % 2
    spot = lambda k, other: (x + k) % (size // 2) * 2 + (y + other) % 2
    order = [(0, 0), (3, 0), (1, 0), (2, 0), (0, 1), (3, 1), (1, 1), (2, 1)]
    order = jnp.stack([spot(*o) for o in order]).astype(jnp.int32)
    peer = jnp.arange(size, dtype=jnp.int32)
    return order, (peer // 2 - x) % (size // 2) * 2 + (peer % 2 != y)


def share_kernel(subs_ref, w_ref, out_ref, sems):
    owners, parts, size, width = out_ref.shape
    copies = []
    for k in range(parts):
        rows = pl.ds(pl.multiple_of(subs_ref[k] * size, size), size)
        for t in range(owners):
            copies.append(
                pltpu.make_async_copy(
                    w_ref.at[rows, t * width : (t + 1) * width], out_ref.at[t, k], sems.at[t, k]
                )
            )
    for copy in copies:
        copy.start()
    for copy in copies:
        copy.wait()


def share_rows(out_weight, subs, size, width):
    owners = out_weight.shape[1] // width
    return pl.pallas_call(
        share_kernel,
        in_specs=[pl.BlockSpec(memory_space=pltpu.SMEM), pl.BlockSpec(memory_space=pltpu.HBM)],
        out_specs=pl.BlockSpec(memory_space=pltpu.VMEM),
        out_shape=jax.ShapeDtypeStruct((owners, subs.shape[0], size, width), BF16),
        scratch_shapes=[pltpu.SemaphoreType.DMA((owners, subs.shape[0]))],
        compiler_params=pltpu.CompilerParams(vmem_limit_bytes=58 * MIB),
        cost_estimate=pl.CostEstimate(flops=0, bytes_accessed=4 * MIB, transcendentals=0),
        name="share_rows",
    )(subs, out_weight)


def weight_first(out_weight, width):
    depth = out_weight.shape[0]
    tensor = out_weight.shape[1] // width
    size = depth // 8
    me = lax.axis_index("dp")
    core, odd = me % 2, me // 2 % 2
    sub_a, sub_b = core * 4 + odd, core * 4 + 3 - odd
    pair = jnp.stack([sub_a, sub_b]).astype(jnp.int32)
    share = share_rows(out_weight, pair, size, width)

    own = [sub_a, sub_b, core * 4 + 1 - odd, core * 4 + 2 + odd]
    return share, jnp.stack(own + [(k + 4) % 8 for k in own]).astype(jnp.int32)


def weight_second(share):
    count = lax.axis_size("dp")
    turn = lambda i, by: i // 8 * 8 + (i + 2 * by) % 8
    z_of = lambda i: i // 2 % 4
    pairs_a = [(i, turn(i, -1 if z_of(i) % 2 else 1)) for i in range(count)]
    pairs_b = [(i, turn(i, 1 if z_of(i) % 2 else -1)) for i in range(count)]
    beside_a = lax.ppermute(share[:, :1], "dp", pairs_a)
    beside_b = lax.ppermute(share[:, 1:], "dp", pairs_b)
    return [share, beside_a, beside_b]


def weight_third(weights):
    cores = [(i, i ^ 1) for i in range(lax.axis_size("dp"))]
    return weights + [lax.ppermute(x, "dp", cores) for x in weights]


def local(
    query,
    new_keys,
    new_values,
    cache_keys,
    cache_values,
    cache_lengths,
    residual,
    out_weight,
    bridge_weight,
    text_table,
    codec_table,
    tokens,
    frames,
    talk_gain,
):
    steps, streams, depth = query.shape
    width = residual.shape[2]
    talk = bridge_weight.shape[1]
    tensor = out_weight.shape[1] // width
    dp = lax.axis_size("dp")
    rows = steps * streams
    per = streams // tensor

    feats = text_table.shape[0]
    shift = (lax.axis_index("dp") * tensor + lax.axis_index("tensor")) * feats % LANES
    shift = shift[None].astype(jnp.int32)
    share, subs = weight_first(out_weight, width)
    ids = jnp.concatenate([tokens, frames], axis=0)
    share, query, ids, spots = gather_ids(ids, share, query)
    share = lax.all_to_all(share, "tensor", 0, 0, tiled=True)

    attended = attention(query, new_keys, new_values, cache_keys, cache_values, cache_lengths)
    attended, ids = lax.optimization_barrier((attended.reshape(rows, depth), ids))
    first = gather_first(attended)
    text = look_up(ids, 0, spots, text_table, shift, tensor)
    text, share = lax.optimization_barrier((text, share))
    weights = weight_second(share)
    emb = look_up(ids, 1, spots, codec_table, shift, tensor, text)
    first, emb = lax.optimization_barrier((first, emb))
    attended = [attended] + first + gather_second(first)
    residual = residual.reshape(steps, tensor, per, width)
    order, owner_spots = peers_order()
    attended, mine, done = collect_rows(attended, order, owner_spots, residual)
    weights, done = lax.optimization_barrier((weights, done))
    emb = lax.all_to_all(emb, BOTH, 0, 0, tiled=True)
    weight = collect_weight(weight_third(weights), subs, done)
    hidden = jnp.dot(attended, weight.reshape(tensor * depth, width), preferred_element_type=F32)
    hidden = (mine.reshape(rows, width).astype(F32) + hidden).astype(BF16)
    parts = bridge_parts(hidden, bridge_weight)
    talker = finish(parts, place(emb, talk), talk_gain.reshape(1, talk))
    hidden = restore(hidden.reshape(tensor, steps, per, width), owner_spots)
    return hidden.reshape(steps, streams, width), talker.reshape(steps, per, talk)


def solution(mesh):
    in_specs = (
        P(None, "dp", "tensor"),
        P(None, "dp", "tensor"),
        P(None, "dp", "tensor"),
        P("dp", None, "tensor"),
        P("dp", None, "tensor"),
        P("dp"),
        P(None, "dp", "tensor"),
        P("tensor", None),
        P("tensor", None),
        P(("dp", "tensor"), None),
        P(("dp", "tensor"), None),
        P(None, "dp"),
        P(None, "dp"),
        P(),
    )
    out_specs = (P(None, "dp", "tensor"), P(None, ("dp", "tensor"), None))
    return jax.shard_map(local, mesh=mesh, in_specs=in_specs, out_specs=out_specs, check_vma=False)
```

```python
import functools

import jax
import jax.numpy as jnp
from jax import lax
from jax.experimental import pallas as pl
from jax.experimental.pallas import tpu as pltpu
from jax.sharding import PartitionSpec as P

QH = 32
KVH = 8
HD = 128
CAP = 64
GROUP = QH // KVH
STEPS = 4
SB = 16
BLOCKS = 2
LANES = 128
FPAD = 32
PACK = LANES // FPAD
UNITS = 8
BF16 = jnp.bfloat16
F32 = jnp.float32
BOTH = ("dp", "tensor")
MIB = 1 << 20


def iota(shape, dim):
    return lax.broadcasted_iota(jnp.int32, shape, dim)


def attention_kernel(len_ref, q_ref, ck_ref, cv_ref, nk_ref, nv_ref, out_ref):
    some = SB // 2
    rows = STEPS * GROUP * some
    scale = 1.0 / HD**0.5
    contract = (((1,), (1,)), ((), ()))
    query = [
        q_ref[t, :, h * HD : (h + 1) * HD].astype(F32) for t in range(STEPS) for h in range(GROUP)
    ]
    fresh = [[ref[t].astype(F32) for t in range(STEPS)] for ref in (nk_ref, nv_ref)]
    own = iota((rows, 1), 0) % some
    start = own * CAP
    spot = iota((rows, some * CAP), 1)
    row, col = iota((rows, STEPS * some), 0), iota((rows, STEPS * some), 1)
    seen = (row % some == col % some) & (col // some <= row // (GROUP * some))
    results = []
    for part in range(2 * BLOCKS):
        here = slice(part * some, (part + 1) * some)
        queries = jnp.concatenate([q[here] for q in query], axis=0).astype(BF16)
        cached_k = ck_ref[here].reshape(some * CAP, HD)
        cached_v = cv_ref[here].reshape(some * CAP, HD)
        fresh_k, fresh_v = [jnp.concatenate([x[here] for x in f], axis=0).astype(BF16) for f in fresh]
        score_c = lax.dot_general(queries, cached_k, contract, preferred_element_type=F32) * scale
        score_n = lax.dot_general(queries, fresh_k, contract, preferred_element_type=F32) * scale
        stop = start + jnp.concatenate([len_ref[here, :1]] * (STEPS * GROUP), axis=0)
        score_c = jnp.where((spot >= start) & (spot < stop), score_c, -1e30)
        score_n = jnp.where(seen, score_n, -1e30)
        top = jnp.maximum(
            jnp.max(score_c, axis=-1, keepdims=True), jnp.max(score_n, axis=-1, keepdims=True)
        )
        exp_c = jnp.exp(score_c - top)
        exp_n = jnp.exp(score_n - top)
        total = jnp.sum(exp_c, axis=-1, keepdims=True) + jnp.sum(exp_n, axis=-1, keepdims=True)
        inverse = 1.0 / total
        weight_c = (exp_c * inverse).astype(BF16)
        weight_n = (exp_n * inverse).astype(BF16)
        attended = jnp.dot(weight_c, cached_v, preferred_element_type=F32)
        results.append(attended + jnp.dot(weight_n, fresh_v, preferred_element_type=F32))
    for t in range(STEPS):
        for h in range(GROUP):
            at = (t * GROUP + h) * some
            for b in range(BLOCKS):
                both = [r[at : at + some] for r in results[2 * b : 2 * b + 2]]
                both = jnp.concatenate(both, axis=0).astype(BF16)
                out_ref[b, t, :, h * HD : (h + 1) * HD] = both


def attention(query, new_keys, new_values, cache_keys, cache_values, cache_lengths):
    steps, streams, width = query.shape
    blocks = streams // SB
    lengths = jnp.broadcast_to(cache_lengths[:, None], (streams, LANES))
    fresh = pl.BlockSpec((steps, BLOCKS * SB, HD), lambda i: (0, i, 0))
    cached = pl.BlockSpec((BLOCKS * SB, CAP, HD), lambda i: (i, 0, 0))
    return pl.pallas_call(
        attention_kernel,
        grid=(blocks // BLOCKS,),
        in_specs=[
            pl.BlockSpec((BLOCKS * SB, LANES), lambda i: (i, 0)),
            pl.BlockSpec((steps, BLOCKS * SB, width), lambda i: (0, i, 0)),
            cached,
            cached,
            fresh,
            fresh,
        ],
        out_specs=pl.BlockSpec((BLOCKS, steps, SB, width), lambda i: (i, 0, 0, 0)),
        out_shape=jax.ShapeDtypeStruct((blocks, steps, SB, width), BF16),
        compiler_params=pltpu.CompilerParams(vmem_limit_bytes=58 * MIB),
        cost_estimate=pl.CostEstimate(flops=8 * 10**9, bytes_accessed=6 * MIB, transcendentals=0),
        name="attention",
    )(lengths, query, cache_keys, cache_values, new_keys, new_values)


def look_kernel(shift_ref, spot_ref, id_ref, table_ref, *refs, group, first, count):
    other_ref = refs[0] if len(refs) == 4 else None
    out_ref, turned, found = refs[-3:]
    feats, entries = table_ref.shape
    rows = 2 * out_ref.shape[1]
    per = rows // STEPS
    batch = found.shape[0] // rows
    pad = jnp.zeros((FPAD - feats, LANES), BF16)
    slot = iota((LANES, LANES), 1) // FPAD

    def turn(begin, amount):
        parts = []
        for k in range(amount):
            at = pl.multiple_of((begin + k) * LANES, LANES)
            parts += [table_ref[:, pl.ds(at, LANES)], pad]
        if amount < PACK:
            parts.append(jnp.zeros(((PACK - amount) * FPAD, LANES), BF16))
        packed = jnp.concatenate(parts, axis=0).T.astype(F32)
        for k in range(amount):
            at = pl.multiple_of((begin + k) * LANES, LANES)
            turned[pl.ds(at, LANES), :] = jnp.where(slot == k, packed, 0.0)

    def turn_units(i, _):
        for u in range(UNITS):
            turn((i * UNITS + u) * PACK, PACK)
        return 0

    blocks = entries // LANES
    loops = blocks // (UNITS * PACK)
    lax.fori_loop(0, loops, turn_units, 0)
    for begin in range(loops * UNITS * PACK, blocks, PACK):
        turn(begin, min(PACK, blocks - begin))

    place = (iota((LANES, LANES), 1) - shift_ref[0]) & (LANES - 1)
    row = iota((LANES, LANES), 0)
    move = (row % FPAD == place % FPAD) & (place // FPAD % 2 == group)
    move = jnp.where(move, 1.0, 0.0).astype(BF16)
    place = (iota((rows // 2, LANES), 1) - shift_ref[0]) & (LANES - 1)

    def look(i, _):
        def find(j, _):
            o = first + i * batch + j
            base = spot_ref[o // (LANES // per)] + o % (LANES // per) * per
            to = pl.multiple_of(j * rows, rows)
            for t in range(STEPS):
                for s in range(per):
                    at = id_ref[base + ((group * STEPS + t) * LANES + s)]
                    found[pl.ds(to + (t * per + s), 1), :] = turned[pl.ds(at, 1), :]
            return 0

        lax.fori_loop(0, batch, find, 0, unroll=4)
        moved = jnp.dot(found[...].astype(BF16), move, preferred_element_type=F32)
        for j in range(batch):
            a = moved[j * rows : j * rows + rows // 2]
            b = moved[j * rows + rows // 2 : (j + 1) * rows]
            both = jnp.where(place < 2 * FPAD, a, b)
            o = first + i * batch + j
            if other_ref is not None:
                both = both + other_ref[o].astype(F32)
            out_ref[o] = both.astype(BF16)
        return 0

    lax.fori_loop(0, count // batch, look, 0)
    for start, stop in ((0, first), (first + count, out_ref.shape[0])):
        if start < stop:
            out_ref[start:stop] = other_ref[start:stop]


def look_up(ids, group, spots, table, shift, owners, first, count, *other):
    groups, _, streams = ids.shape
    rows = streams * STEPS // owners
    vmem = pl.BlockSpec(memory_space=pltpu.VMEM)
    smem = pl.BlockSpec(memory_space=pltpu.SMEM)
    return pl.pallas_call(
        functools.partial(look_kernel, group=group, first=first, count=count),
        in_specs=[smem, smem, smem, vmem] + [vmem] * len(other),
        out_specs=vmem,
        out_shape=jax.ShapeDtypeStruct((groups * owners, rows // 2, LANES), BF16),
        scratch_shapes=[
            pltpu.VMEM((table.shape[1], LANES), F32),
            pltpu.VMEM((32 * rows, LANES), F32),
        ],
        compiler_params=pltpu.CompilerParams(vmem_limit_bytes=(table.shape[1] // 2048 + 14) * MIB),
        cost_estimate=pl.CostEstimate(
            flops=0, bytes_accessed=table.shape[1] // 1000 * MIB, transcendentals=0
        ),
        name="look_up",
    )(shift, spots, ids.reshape(-1), table, *other)


def collect_rows_kernel(order_ref, spot_ref, *refs, owners):
    a_refs = refs[:owners]
    res_ref, a_all, res_all, done, a_sem, res_sem = refs[owners:]
    rows, depth = a_refs[0].shape
    size = rows // owners
    copies = []
    for b in range(owners):
        to = pl.ds(pl.multiple_of(spot_ref[b] * size, size), size)
        for k in range(owners):
            at = pl.multiple_of(order_ref[k] * depth, depth)
            source = a_refs[k].at[b * size : (b + 1) * size]
            target = a_all.at[to, pl.ds(at, depth)]
            copies.append(pltpu.make_async_copy(source, target, a_sem.at[b, k]))
        for t in range(STEPS):
            target = res_all.at[spot_ref[b], t]
            copies.append(pltpu.make_async_copy(res_ref.at[t, b], target, res_sem.at[b, t]))
    for copy in copies:
        copy.start()
    for copy in copies:
        copy.wait()
    done[...] = jnp.zeros_like(done)


def collect_rows(attended, order, spots, residual):
    owners = len(attended)
    rows, depth = attended[0].shape
    width = residual.shape[-1]
    vmem = pl.BlockSpec(memory_space=pltpu.VMEM)
    smem = pl.BlockSpec(memory_space=pltpu.SMEM)
    return pl.pallas_call(
        functools.partial(collect_rows_kernel, owners=owners),
        in_specs=[smem, smem] + [pl.BlockSpec(memory_space=pl.ANY)] * (owners + 1),
        out_specs=[vmem] * 3,
        out_shape=[
            jax.ShapeDtypeStruct((rows, owners * depth), BF16),
            jax.ShapeDtypeStruct((owners, STEPS, rows // STEPS // owners, width), BF16),
            jax.ShapeDtypeStruct((8, LANES), F32),
        ],
        scratch_shapes=[pltpu.SemaphoreType.DMA((owners, n)) for n in (owners, STEPS)],
        compiler_params=pltpu.CompilerParams(vmem_limit_bytes=58 * MIB),
        cost_estimate=pl.CostEstimate(flops=0, bytes_accessed=8 * MIB, transcendentals=0),
        name="collect_rows",
    )(order, spots, *attended, residual)


def restore_kernel(spot_ref, x_ref, out_ref, sems):
    steps, owners = out_ref.shape[:2]
    copies = [
        pltpu.make_async_copy(x_ref.at[spot_ref[b], t], out_ref.at[t, b], sems.at[b, t])
        for b in range(owners)
        for t in range(steps)
    ]
    for copy in copies:
        copy.start()
    for copy in copies:
        copy.wait()


def restore(x, spots):
    owners, steps, per, width = x.shape
    anywhere = pl.BlockSpec(memory_space=pl.ANY)
    return pl.pallas_call(
        restore_kernel,
        in_specs=[pl.BlockSpec(memory_space=pltpu.SMEM), anywhere],
        out_specs=anywhere,
        out_shape=jax.ShapeDtypeStruct((steps, owners, per, width), x.dtype),
        scratch_shapes=[pltpu.SemaphoreType.DMA((owners, steps))],
        compiler_params=pltpu.CompilerParams(vmem_limit_bytes=12 * MIB),
        cost_estimate=pl.CostEstimate(flops=0, bytes_accessed=2 * MIB, transcendentals=0),
        name="restore",
    )(spots, x)


def collect_weight_kernel(subs_ref, done_ref, *refs):
    del done_ref
    *w_refs, w_all, sems = refs
    copies = []
    for w_ref in w_refs:
        for k in range(w_ref.shape[1]):
            sub = len(copies)
            copies.append(
                pltpu.make_async_copy(w_ref.at[:, k], w_all.at[:, subs_ref[sub]], sems.at[sub])
            )
    for copy in copies:
        copy.start()
    for copy in copies:
        copy.wait()


def collect_weight(weights, subs, done):
    owners, _, size, width = weights[0].shape
    parts = subs.shape[0]
    return pl.pallas_call(
        collect_weight_kernel,
        in_specs=[pl.BlockSpec(memory_space=pltpu.SMEM)]
        + [pl.BlockSpec(memory_space=pl.ANY)] * (len(weights) + 1),
        out_specs=pl.BlockSpec(memory_space=pltpu.VMEM),
        out_shape=jax.ShapeDtypeStruct((owners, parts, size, width), BF16),
        scratch_shapes=[pltpu.SemaphoreType.DMA((parts,))],
        compiler_params=pltpu.CompilerParams(vmem_limit_bytes=12 * MIB),
        cost_estimate=pl.CostEstimate(flops=0, bytes_accessed=10 * MIB, transcendentals=0),
        name="collect_weight",
    )(subs, done, *weights)


def place_kernel(emb_ref, out_ref, *, feats):
    holders, half, _ = emb_ref.shape
    lane = iota((half, LANES), 1)
    for tile in range(holders * feats // LANES):
        start = tile * LANES
        found = [jnp.zeros((half, LANES), F32) for _ in range(PACK)]
        for h in range(start // feats, min((start + LANES - 1) // feats, holders - 1) + 1):
            row = emb_ref[h].astype(F32)
            low, high = max(h * feats - start, 0), min((h + 1) * feats - start, LANES)
            for g in range(PACK):
                spot = (lane - g * FPAD) & (LANES - 1)
                found[g] = jnp.where((spot >= low) & (spot < high), row, found[g])
        a = found[0] + pltpu.roll(found[1], LANES - FPAD, 1)
        b = found[2] + pltpu.roll(found[3], LANES - FPAD, 1)
        b = pltpu.roll(b, LANES // 2, 1)
        out_ref[:half, start : start + LANES] = a
        out_ref[half:, start : start + LANES] = b


def place(emb, talk):
    holders, half, _ = emb.shape
    blocks = 4
    return pl.pallas_call(
        functools.partial(place_kernel, feats=talk // holders),
        grid=(blocks,),
        in_specs=[pl.BlockSpec((holders // blocks, half, LANES), lambda i: (i, 0, 0))],
        out_specs=pl.BlockSpec((2 * half, talk // blocks), lambda i: (0, i)),
        out_shape=jax.ShapeDtypeStruct((2 * half, talk), F32),
        compiler_params=pltpu.CompilerParams(vmem_limit_bytes=8 * MIB),
        cost_estimate=pl.CostEstimate(flops=0, bytes_accessed=8 * MIB, transcendentals=0),
        name="place",
    )(emb)


def finish_kernel(*refs):
    *part_refs, emb_ref, gain_ref, out_ref, mixed = refs
    rows, talk = out_ref.shape
    halves = [part_refs[: len(part_refs) // 2], part_refs[len(part_refs) // 2 :]]
    square = jnp.zeros((rows, LANES), F32)
    for c in range(talk // LANES):
        cols = slice(c * LANES, (c + 1) * LANES)
        half, at = divmod(c * LANES, talk // 2)
        total = emb_ref[:, cols]
        for ref in halves[half]:
            total = total + ref[:rows, at : at + LANES].astype(F32)
        mixed[:, cols] = total
        square = square + total * total
    mean = jnp.sum(square, axis=-1, keepdims=True) * (1.0 / talk)
    factor = lax.rsqrt(mean + 1e-06)
    for c in range(talk // LANES):
        cols = slice(c * LANES, (c + 1) * LANES)
        gain = gain_ref[:, cols].astype(F32)
        out_ref[:, cols] = (mixed[:, cols] * factor * gain).astype(BF16)


def finish(parts, emb, gain):
    rows, talk = emb.shape
    vmem = pl.BlockSpec(memory_space=pltpu.VMEM)
    return pl.pallas_call(
        finish_kernel,
        in_specs=[vmem] * (len(parts) + 2),
        out_specs=vmem,
        out_shape=jax.ShapeDtypeStruct((rows, talk), BF16),
        scratch_shapes=[pltpu.VMEM((rows, talk), F32)],
        compiler_params=pltpu.CompilerParams(vmem_limit_bytes=8 * MIB),
        cost_estimate=pl.CostEstimate(flops=0, bytes_accessed=8 * MIB, transcendentals=0),
        name="finish",
    )(*parts, emb, gain)


def bridge_parts(hidden, bridge_weight):
    up, down, _, across = tensor_pairs()
    talk = bridge_weight.shape[1]
    rows = hidden.shape[0] // 4
    own = rows // 2

    def product(block, half):
        weight = bridge_weight[:, half * (talk // 2) : (half + 1) * (talk // 2)]
        block = hidden[block * rows : (block + 1) * rows]
        return jnp.dot(block, weight, preferred_element_type=F32)

    by_up = send(product(2, 0).astype(BF16), up)
    by_down = send(product(2, 1).astype(BF16), down)
    from_down = [send(product(3, 0).astype(BF16), down)]
    from_up = [None, send(product(1, 1).astype(BF16), up)]
    from_up[0] = send((product(1, 0) + by_up.astype(F32)).astype(BF16), up)
    from_down.append(send((product(3, 1) + by_down.astype(F32)).astype(BF16), down))
    parts = []
    for half in range(2):
        mine = product(0, half)
        other = mine[own:] + from_up[half][own:].astype(F32) + from_down[half][own:].astype(F32)
        parts += [mine, from_up[half], from_down[half], send(other.astype(BF16), across)]
    return parts


def gather_ids(ids, share, later):
    count = lax.axis_size("dp")
    size = ids.size
    get = lambda x, peer: lax.ppermute(x, "dp", [(peer(i), i) for i in range(count)])
    turn = lambda by: lambda i: i // 8 * 8 + (i + 2 * by) % 8
    across_y, share = lax.optimization_barrier((get(ids, lambda i: i ^ 8), share))
    ids = jnp.stack([ids, across_y])
    ids = jnp.concatenate([ids, get(ids, lambda i: i ^ 1)])
    ids, later = lax.optimization_barrier((ids, later))
    ids = jnp.concatenate([ids] + [get(ids, turn(by)) for by in (1, 2, 3)])
    me = lax.axis_index("dp")
    peer = jnp.arange(count, dtype=jnp.int32)
    across = (peer // 2 - me // 2) % 4
    other = (peer % 2 != me % 2) * 2 + (peer // 8 != me // 8)
    return share, later, ids, ((across * 4 + other) * size).astype(jnp.int32)


def tensor_pairs():
    size = lax.axis_size("tensor")
    along = lambda by: [(i, (i + 2 * by) % size) for i in range(size)]
    return along(1), along(-1), along(2), [(i, i ^ 1) for i in range(size)]


def send(x, pairs):
    return lax.ppermute(x, "tensor", pairs)


def gather_first(own):
    return [send(own, pairs) for pairs in tensor_pairs()]


def gather_second(first):
    up, down, _, across = tensor_pairs()
    _, _, far, beside = first
    return [send(beside, up), send(beside, down), send(far, across)]


def peers_order():
    size = lax.axis_size("tensor")
    me = lax.axis_index("tensor")
    x, y = me // 2, me % 2
    spot = lambda k, other: (x + k) % (size // 2) * 2 + (y + other) % 2
    order = [(0, 0), (3, 0), (1, 0), (2, 0), (0, 1), (3, 1), (1, 1), (2, 1)]
    order = jnp.stack([spot(*o) for o in order]).astype(jnp.int32)
    peer = jnp.arange(size, dtype=jnp.int32)
    return order, (peer // 2 - x) % (size // 2) * 2 + (peer % 2 != y)


def share_kernel(subs_ref, w_ref, out_ref, sems):
    owners, parts, size, width = out_ref.shape
    copies = []
    for k in range(parts):
        rows = pl.ds(pl.multiple_of(subs_ref[k] * size, size), size)
        for t in range(owners):
            copies.append(
                pltpu.make_async_copy(
                    w_ref.at[rows, t * width : (t + 1) * width], out_ref.at[t, k], sems.at[t, k]
                )
            )
    for copy in copies:
        copy.start()
    for copy in copies:
        copy.wait()


def share_rows(out_weight, subs, size, width):
    owners = out_weight.shape[1] // width
    return pl.pallas_call(
        share_kernel,
        in_specs=[pl.BlockSpec(memory_space=pltpu.SMEM), pl.BlockSpec(memory_space=pltpu.HBM)],
        out_specs=pl.BlockSpec(memory_space=pltpu.VMEM),
        out_shape=jax.ShapeDtypeStruct((owners, subs.shape[0], size, width), BF16),
        scratch_shapes=[pltpu.SemaphoreType.DMA((owners, subs.shape[0]))],
        compiler_params=pltpu.CompilerParams(vmem_limit_bytes=58 * MIB),
        cost_estimate=pl.CostEstimate(flops=0, bytes_accessed=4 * MIB, transcendentals=0),
        name="share_rows",
    )(subs, out_weight)


def weight_first(out_weight, width):
    depth = out_weight.shape[0]
    tensor = out_weight.shape[1] // width
    size = depth // 8
    me = lax.axis_index("dp")
    core, odd = me % 2, me // 2 % 2
    sub_a, sub_b = core * 4 + odd, core * 4 + 3 - odd
    pair = jnp.stack([sub_a, sub_b]).astype(jnp.int32)
    share = share_rows(out_weight, pair, size, width)

    own = [sub_a, sub_b, core * 4 + 1 - odd, core * 4 + 2 + odd]
    return share, jnp.stack(own + [(k + 4) % 8 for k in own]).astype(jnp.int32)


def weight_second(share):
    count = lax.axis_size("dp")
    turn = lambda i, by: i // 8 * 8 + (i + 2 * by) % 8
    z_of = lambda i: i // 2 % 4
    pairs_a = [(i, turn(i, -1 if z_of(i) % 2 else 1)) for i in range(count)]
    pairs_b = [(i, turn(i, 1 if z_of(i) % 2 else -1)) for i in range(count)]
    beside_a = lax.ppermute(share[:, :1], "dp", pairs_a)
    beside_b = lax.ppermute(share[:, 1:], "dp", pairs_b)
    return [share, beside_a, beside_b]


def weight_third(weights):
    cores = [(i, i ^ 1) for i in range(lax.axis_size("dp"))]
    return weights + [lax.ppermute(x, "dp", cores) for x in weights]


def local(
    query,
    new_keys,
    new_values,
    cache_keys,
    cache_values,
    cache_lengths,
    residual,
    out_weight,
    bridge_weight,
    text_table,
    codec_table,
    tokens,
    frames,
    talk_gain,
):
    steps, streams, depth = query.shape
    width = residual.shape[2]
    talk = bridge_weight.shape[1]
    tensor = out_weight.shape[1] // width
    dp = lax.axis_size("dp")
    rows = steps * streams
    per = streams // tensor

    feats = text_table.shape[0]
    shift = (lax.axis_index("dp") * tensor + lax.axis_index("tensor")) * feats % LANES
    shift = shift[None].astype(jnp.int32)
    share, subs = weight_first(out_weight, width)
    ids = jnp.concatenate([tokens, frames], axis=0)
    share, query, ids, spots = gather_ids(ids, share, query)
    share = lax.all_to_all(share, "tensor", 0, 0, tiled=True)

    attended = attention(query, new_keys, new_values, cache_keys, cache_values, cache_lengths)
    attended, ids = lax.optimization_barrier((attended.reshape(rows, depth), ids))
    first = gather_first(attended)
    text = look_up(ids, 0, spots, text_table, shift, tensor, 0, dp * tensor)
    text, share = lax.optimization_barrier((text, share))
    weights = weight_second(share)
    half = dp * tensor // 2
    emb = look_up(ids, 1, spots, codec_table, shift, tensor, 0, half, text)
    first, emb = lax.optimization_barrier((first, emb))
    attended = [attended] + first + gather_second(first)
    emb = look_up(ids, 1, spots, codec_table, shift, tensor, half, half, emb)
    residual = residual.reshape(steps, tensor, per, width)
    order, owner_spots = peers_order()
    attended, mine, done = collect_rows(attended, order, owner_spots, residual)
    weights, done, emb = lax.optimization_barrier((weights, done, emb))
    emb = lax.all_to_all(emb, BOTH, 0, 0, tiled=True)
    weight = collect_weight(weight_third(weights), subs, done)
    hidden = jnp.dot(attended, weight.reshape(tensor * depth, width), preferred_element_type=F32)
    hidden = (mine.reshape(rows, width).astype(F32) + hidden).astype(BF16)
    parts = bridge_parts(hidden, bridge_weight)
    talker = finish(parts, place(emb, talk), talk_gain.reshape(1, talk))
    hidden = restore(hidden.reshape(tensor, steps, per, width), owner_spots)
    return hidden.reshape(steps, streams, width), talker.reshape(steps, per, talk)


def solution(mesh):
    in_specs = (
        P(None, "dp", "tensor"),
        P(None, "dp", "tensor"),
        P(None, "dp", "tensor"),
        P("dp", None, "tensor"),
        P("dp", None, "tensor"),
        P("dp"),
        P(None, "dp", "tensor"),
        P("tensor", None),
        P("tensor", None),
        P(("dp", "tensor"), None),
        P(("dp", "tensor"), None),
        P(None, "dp"),
        P(None, "dp"),
        P(),
    )
    out_specs = (P(None, "dp", "tensor"), P(None, ("dp", "tensor"), None))
    return jax.shard_map(local, mesh=mesh, in_specs=in_specs, out_specs=out_specs, check_vma=False)
```
